32 devices in a mesh: section: 2 (over core), fsdp: 16 (over z, y, x).
Axes of the slice: x: 2, y: 2, z: 4, core: 2. Of those that a mesh axis runs over, the one named last changes fastest.
Arguments:
- ends: bfloat16 [2, 2, 2048, 576], P('section', None, 'fsdp'), may hold values from -6 to 6
- weights: bfloat16 [2, 3538944], P('section', 'fsdp'), may hold values from -4 to 4
- gains: bfloat16 [2, 1152], P('section', 'fsdp'), may hold values from 0.5 to 1.5
- segments: int32 [2, 2048], P(None, 'fsdp'), may hold values from 0 to 15, never falling along the last dimension, each value on 1 to 256 neighbouring positions
Outputs:
- ends_out: bfloat16 [2, 2, 2048, 576], P('section', None, 'fsdp')
- weight_grads: float32 [2, 3538944], P('section', 'fsdp')
- gain_grads: float32 [2, 1152], P('section', 'fsdp')
The draws below stay inside these ranges and needn't reach their ends.
Inputs may be any that keep to these rules, and one draw needn't show every extreme that they name: `segments`: segment numbers never fall along a micro-batch and each of 0 to 15 is used; a document holds at most 256 tokens, one in each micro-batch exactly 256.
All inputs are finite; a program needn't handle non-finite values.
Results may differ from the reference program's by a relative error of at most 0.023.
Values may be sent and summed in bfloat16 or wider, within the bound.
No kernel may reach another device: no remote copies, remote signals or barrier semaphores. Data moves between devices by JAX's collectives and lax.ppermute only.
A program may use at most 128 MiB of HBM per device.

```python
import math
import jax
import jax.numpy as jnp
import numpy as np
from jax import lax

D = 576
HEADS = 9
KV_HEADS = 3
HEAD = 64
FF = 1536
MICRO = 2
TOKENS = 2048
DOC_MOST = 256
SEGS = 16


def draw_weights(key, part):
    key = jax.random.fold_in(key, 11)
    query_cols = HEADS * HEAD
    kv_cols = KV_HEADS * HEAD
    lengths = [D * query_cols, D * kv_cols, D * kv_cols, query_cols * D, D * FF, D * FF, FF * D]
    scales = [1.5 * D ** (-0.5), D ** (-0.5), D ** (-0.5), 4.0 * query_cols ** (-0.5), D ** (-0.5), D ** (-0.5), FF ** (-0.5)]
    total = sum(lengths)
    index = jnp.arange(total, dtype=jnp.int32)
    scale_row = jnp.zeros((total,), jnp.float32)
    offset = 0
    for length, factor in zip(lengths, scales):
        scale_row = jnp.where((index >= offset) & (index < offset + length), factor, scale_row)
        offset = offset + length
    base = jnp.clip(jax.random.normal(key, (2, total), jnp.float32), -4.0, 4.0)
    return (base * scale_row[None, :]).astype(jnp.bfloat16)


def levels(key, shape, shards, least, largest):
    level = 1.0
    for dim, blocks in shards:
        steps = jax.random.uniform(jax.random.fold_in(jax.random.fold_in(key, 6), dim), (blocks,), jnp.float32, least / len(shards), largest / len(shards))
        level = level * jnp.repeat(jnp.exp(steps), shape[dim] // blocks).reshape((-1,) + (1,) * (len(shape) - 1 - dim))
    return level


def profile(amount, total, most, skew):
    portions = [(1 << 20) // math.isqrt(rank ** skew) + 1 for rank in range(2, amount + 1)]
    rest, counts = total - most - (amount - 1), [1] * (amount - 1)
    while rest > 0:
        movable = [i for i in range(amount - 1) if counts[i] < most]
        whole, budget = sum([portions[i] for i in movable]), rest
        for i in movable:
            addition = min(most - counts[i], max(1, budget * portions[i] // whole), rest)
            counts[i] = counts[i] + addition
            rest = rest - addition
    return np.array([most] + counts)


def uneven(stream_key, number_of, total, most, slope):
    if number_of == 2:
        one = jax.random.randint(stream_key, (), max(1, total - most), min(most, total - 1) + 1)
        return jnp.stack([one, total - one])
    sizes = jnp.asarray(profile(number_of, total, most, slope), jnp.int32)
    pairs = (number_of - 1) // 2
    donor, sink = sizes[1:1 + 2 * pairs:2], sizes[2:2 + 2 * pairs:2]
    slack = jnp.minimum(donor - 1, most - sink)
    moved = jax.random.randint(jax.random.fold_in(stream_key, 1), (pairs,), 0, 1 << 20) % (slack + 1)
    sizes = sizes.at[1:1 + 2 * pairs:2].set(donor - moved).at[2:2 + 2 * pairs:2].set(sink + moved)
    return sizes[jax.random.permutation(jax.random.fold_in(stream_key, 2), number_of)]


def centred(stream_key, shape, scale, reach, cuts=(), kind=jnp.bfloat16):
    array = scale * jax.random.normal(stream_key, shape, jnp.float32)
    if cuts:
        array = array * levels(stream_key, shape, cuts, -0.22, 0.18)
    return jnp.clip(array, -reach, reach).astype(kind)


def setup_inputs(seed: int = 0) -> dict:
    key_list = jax.random.split(jax.random.key(seed), 5)
    return {
        "ends": centred(key_list[0], (2, MICRO, TOKENS, D), 1.0, 6.0, ((0, 2), (2, 16))),
        "weights": draw_weights(jax.random.fold_in(key_list[4], 71), 0),
        "gains": jnp.clip(1.0 + 0.1 * jax.random.normal(key_list[2], (2, 2 * D), jnp.float32), 0.5, 1.5).astype(jnp.bfloat16),
        "segments": jax.vmap(lambda own: jnp.searchsorted(jnp.cumsum(uneven(own, SEGS, TOKENS, DOC_MOST, 0)), jnp.arange(TOKENS), side="right"))(jax.random.split(key_list[3], MICRO)).reshape((MICRO, TOKENS)).astype(jnp.int32),
    }


epsilon = 1e-05
rope_base = 100000.0
masked_score = -1e+30

@jax.custom_vjp
def low(v):
    return lax.optimization_barrier(v.astype(jnp.bfloat16)).astype(jnp.float32)

@jax.custom_vjp
def low_back(v):
    return v

def low_keep(v):
    return (low(v), None)

def low_pass(kept, grad):
    return (grad,)

def back_keep(v):
    return (v, None)

def back_low(kept, grad):
    return (low(grad),)
low.defvjp(low_keep, low_pass)
low_back.defvjp(back_keep, back_low)

def product(left, right):
    return jnp.dot(left, right, preferred_element_type=jnp.float32, precision=lax.Precision.HIGHEST)

def unpack(flat_vector):
    query_cols = HEADS * HEAD
    kv_cols = KV_HEADS * HEAD
    shapes = [(D, query_cols), (D, kv_cols), (D, kv_cols), (query_cols, D), (D, FF), (D, FF), (FF, D)]
    pieces = []
    offset = 0
    for row_count, col_count in shapes:
        pieces.append(flat_vector[offset:offset + row_count * col_count].reshape(row_count, col_count))
        offset = offset + row_count * col_count
    return pieces

def positions_of(segment):
    length = segment.shape[0]
    index = jnp.arange(length, dtype=jnp.int32)
    change = jnp.concatenate([jnp.ones((1,), dtype=bool), segment[1:] != segment[:-1]])
    starts = lax.cummax(jnp.where(change, index, 0), axis=0)
    return index - starts

def rope_tables(positions):
    half = HEAD // 2
    frequency = rope_base ** (-2.0 * jnp.arange(half, dtype=jnp.float32) / HEAD)
    angles = positions.astype(jnp.float32)[:, None] * frequency[None, :]
    return (jnp.cos(angles), jnp.sin(angles))

def rotate(values, cosine, sine):
    half = values.shape[-1] // 2
    front = values[..., :half]
    back = values[..., half:]
    cos_row = cosine[:, None, :]
    sin_row = sine[:, None, :]
    return jnp.concatenate([front * cos_row - back * sin_row, back * cos_row + front * sin_row], axis=-1)

def attention(queries, keys, values, segment):
    length = queries.shape[0]
    block = math.gcd(length, 512)
    count = length // block
    group = HEADS // KV_HEADS
    scale = HEAD ** (-0.5)
    keys_pad = jnp.pad(keys, ((DOC_MOST, 0), (0, 0), (0, 0)))
    values_pad = jnp.pad(values, ((DOC_MOST, 0), (0, 0), (0, 0)))
    segment_pad = jnp.concatenate([jnp.full((DOC_MOST,), -1, jnp.int32), segment])
    query_blocks = queries.reshape(count, block, KV_HEADS, group, HEAD)
    segment_blocks = segment.reshape(count, block)

    @jax.checkpoint
    def one_block(inputs):
        query_block, segment_block, number = inputs
        start = number * block
        key_block = lax.dynamic_slice_in_dim(keys_pad, start, DOC_MOST + block, 0)
        value_block = lax.dynamic_slice_in_dim(values_pad, start, DOC_MOST + block, 0)
        key_segment = lax.dynamic_slice_in_dim(segment_pad, start, DOC_MOST + block, 0)
        scores = low_back(jnp.einsum('qkgd,wkd->kgqw', query_block, key_block, precision=lax.Precision.HIGHEST) * scale)
        query_place = jnp.arange(block, dtype=jnp.int32)[:, None] + DOC_MOST
        key_place = jnp.arange(DOC_MOST + block, dtype=jnp.int32)[None, :]
        allowed = (segment_block[:, None] == key_segment[None, :]) & (key_place <= query_place)
        scores = jnp.where(allowed[None, None], scores, masked_score)
        top = lax.optimization_barrier(jnp.max(scores, axis=-1, keepdims=True))
        powers = jnp.exp(scores - top)
        shares = low(powers / lax.optimization_barrier(jnp.sum(powers, axis=-1, keepdims=True)))
        mixed = jnp.einsum('kgqw,wkd->qkgd', shares, value_block, precision=lax.Precision.HIGHEST)
        return mixed.reshape(block, HEADS * HEAD)
    outputs = lax.map(one_block, (query_blocks, segment_blocks, jnp.arange(count, dtype=jnp.int32)))
    return outputs.reshape(length, HEADS * HEAD)

def layer(states, flat_vector, gain_vector, segment, cosine, sine):
    w_query, w_key, w_value, w_out, w_gate, w_up, w_down = unpack(flat_vector)
    gain_one = gain_vector[:D]
    gain_two = gain_vector[D:]
    length = states.shape[0]
    normed = low(states * lax.rsqrt(lax.optimization_barrier(jnp.mean(states * states, axis=-1, keepdims=True)) + epsilon) * gain_one)
    queries = low_back(product(normed, w_query)).reshape(length, HEADS, HEAD)
    keys = low_back(product(normed, w_key)).reshape(length, KV_HEADS, HEAD)
    values = low(low_back(product(normed, w_value))).reshape(length, KV_HEADS, HEAD)
    queries = low(rotate(queries, cosine, sine)).reshape(length, KV_HEADS, HEADS // KV_HEADS, HEAD)
    keys = low(rotate(keys, cosine, sine))
    attended = low(low_back(attention(queries, keys, values, segment)))
    mixed = states + low_back(product(attended, w_out))
    normed_two = low(mixed * lax.rsqrt(lax.optimization_barrier(jnp.mean(mixed * mixed, axis=-1, keepdims=True)) + epsilon) * gain_two)
    gate = low_back(product(normed_two, w_gate))
    up_part = low_back(product(normed_two, w_up))
    hidden = low(jax.nn.silu(gate) * up_part)
    return mixed + product(hidden, w_down)

def reference(ends, weights, gains, segments):
    weight_all = weights.astype(jnp.float32)
    gain_all = gains.astype(jnp.float32)

    def one_micro(totals, inputs):
        first_input, cotangent, segment = inputs
        cosine, sine = rope_tables(positions_of(segment))

        def forward(states, weight_vectors, gain_vectors):
            middle = layer(states, weight_vectors[0], gain_vectors[0], segment, cosine, sine)
            middle = low_back(low(middle))
            return layer(middle, weight_vectors[1], gain_vectors[1], segment, cosine, sine)
        output, pullback = jax.vjp(forward, first_input.astype(jnp.float32), weight_all, gain_all)
        grad_input, grad_weights, grad_gains = pullback(cotangent.astype(jnp.float32))
        return ((totals[0] + grad_weights, totals[1] + grad_gains), (grad_input.astype(jnp.bfloat16), output.astype(jnp.bfloat16)))
    start = (jnp.zeros_like(weight_all), jnp.zeros_like(gain_all))
    totals, (grad_inputs, outputs) = lax.scan(one_micro, start, (ends[0], ends[1], segments))
    return (jnp.stack([grad_inputs, outputs]), totals[0], totals[1])
```

```python
import jax
import jax.numpy as jnp
from jax import lax
from jax.experimental import pallas as pl
from jax.experimental.pallas import tpu as pltpu
from jax.sharding import PartitionSpec as P

D = 576
HEADS = 9
KV_HEADS = 3
HEAD = 64
FF = 1536
REACH = 2


epsilon = 1e-05
rope_base = 100000.0
masked_score = -1e30


def passed_along(value, axis, steps):
    count = lax.axis_size(axis)
    first, last = (max(0, -steps), min(count, count - steps))
    return lax.ppermute(value, axis, [(source, source + steps) for source in range(first, last)])


def rope_tables(positions):
    half = HEAD // 2
    frequency = rope_base ** (-2.0 * jnp.arange(half, dtype=jnp.float32) / HEAD)
    angles = positions.astype(jnp.float32)[:, None] * frequency[None, :]
    return (jnp.cos(angles), jnp.sin(angles))


def rotate(values, cosine, sine):
    half = values.shape[-1] // 2
    front = values[..., :half]
    back = values[..., half:]
    cos_row = cosine[:, None, :]
    sin_row = sine[:, None, :]
    return jnp.concatenate(
        [front * cos_row - back * sin_row, back * cos_row + front * sin_row], axis=-1
    )


def rotate_back(values, cosine, sine):
    half = values.shape[-1] // 2
    front = values[..., :half]
    back = values[..., half:]
    cos_row = cosine[:, None, :]
    sin_row = sine[:, None, :]
    return jnp.concatenate(
        [front * cos_row + back * sin_row, back * cos_row - front * sin_row], axis=-1
    )


def rms_scale(states):
    return lax.rsqrt(jnp.mean(states * states, axis=-1, keepdims=True) + epsilon)


def rms_back(states, scale, gain, grad):
    weighted = grad * gain
    return scale * weighted - states * (scale * scale * scale) * jnp.mean(
        weighted * states, axis=-1, keepdims=True
    )


def unpack(flat_vector):
    query_cols = HEADS * HEAD
    kv_cols = KV_HEADS * HEAD
    shapes = [
        (D, query_cols),
        (D, kv_cols),
        (D, kv_cols),
        (query_cols, D),
        (D, FF),
        (D, FF),
        (FF, D),
    ]
    pieces = []
    offset = 0
    for row_count, col_count in shapes:
        pieces.append(
            flat_vector[offset : offset + row_count * col_count].reshape(row_count, col_count)
        )
        offset = offset + row_count * col_count
    return pieces


def select(first, one, other):
    return jax.tree.map(lambda left, right: jnp.where(first, left, right), one, other)


def key_window(pair):
    pieces = [pair]
    for reach in range(1, REACH + 1):
        pieces.insert(0, passed_along(pair, "fsdp", reach))
    return jnp.concatenate(pieces, axis=0)


def attend_forward(queries, keys_win, values_win, allowed):
    scores = jnp.einsum(
        "qkgd,wkd->kgqw", queries, keys_win, preferred_element_type=jnp.float32
    ) * HEAD ** (-0.5)
    scores = jnp.where(allowed[None, None], scores, masked_score)
    top = jnp.max(scores, axis=-1, keepdims=True)
    powers = jnp.exp(scores - top)
    total = jnp.sum(powers, axis=-1, keepdims=True)
    shares_low = (powers / total).astype(jnp.bfloat16)
    attended = jnp.einsum(
        "kgqw,wkd->qkgd", shares_low, values_win, preferred_element_type=jnp.float32
    )
    return (attended, top + jnp.log(total))


def attend_backward(queries, keys_win, values_win, allowed, log_total, grad_attended):
    scale = HEAD ** (-0.5)
    scores = (
        jnp.einsum("qkgd,wkd->kgqw", queries, keys_win, preferred_element_type=jnp.float32) * scale
    )
    scores = jnp.where(allowed[None, None], scores, masked_score)
    shares = jnp.exp(scores - log_total)
    shares_low = shares.astype(jnp.bfloat16)
    grad_shares = jnp.einsum(
        "qkgd,wkd->kgqw", grad_attended, values_win, preferred_element_type=jnp.float32
    )
    inner = jnp.sum(shares * grad_shares, axis=-1, keepdims=True)
    grad_scores = (shares * (grad_shares - inner)).astype(jnp.bfloat16)
    grad_query = (
        jnp.einsum("kgqw,wkd->qkgd", grad_scores, keys_win, preferred_element_type=jnp.float32)
        * scale
    )
    grad_keys = (
        jnp.einsum("kgqw,qkgd->wkd", grad_scores, queries, preferred_element_type=jnp.float32)
        * scale
    )
    grad_values = jnp.einsum(
        "kgqw,qkgd->wkd", shares_low, grad_attended, preferred_element_type=jnp.float32
    )
    return (grad_query, grad_keys, grad_values)


def layer_forward(states, mats, gain_pair, table):
    w_query, w_key, w_value, w_out, w_gate, w_up, w_down = mats
    cosine, sine, allowed = table
    rows = states.shape[0]
    group = HEADS // KV_HEADS
    kv_width = KV_HEADS * HEAD
    scale_one = rms_scale(states)
    normed_low = (states * scale_one * gain_pair[:D]).astype(jnp.bfloat16)
    queries = jnp.dot(normed_low, w_query, preferred_element_type=jnp.float32).reshape(
        rows, HEADS, HEAD
    )
    keys = jnp.dot(normed_low, w_key, preferred_element_type=jnp.float32).reshape(
        rows, KV_HEADS, HEAD
    )
    values = jnp.dot(normed_low, w_value, preferred_element_type=jnp.float32)
    query_low = (
        rotate(queries, cosine, sine).astype(jnp.bfloat16).reshape(rows, KV_HEADS, group, HEAD)
    )
    key_low = rotate(keys, cosine, sine).reshape(rows, kv_width).astype(jnp.bfloat16)
    pair = jnp.concatenate([key_low, values.astype(jnp.bfloat16)], axis=1)
    window = key_window(pair)
    span = window.shape[0]
    keys_win = window[:, :kv_width].reshape(span, KV_HEADS, HEAD)
    values_win = window[:, kv_width:].reshape(span, KV_HEADS, HEAD)
    attended, log_total = attend_forward(query_low, keys_win, values_win, allowed)
    attended_low = attended.reshape(rows, HEADS * HEAD).astype(jnp.bfloat16)
    mixed = states + jnp.dot(attended_low, w_out, preferred_element_type=jnp.float32)
    scale_two = rms_scale(mixed)
    normed_two_low = (mixed * scale_two * gain_pair[D:]).astype(jnp.bfloat16)
    gate = jnp.dot(normed_two_low, w_gate, preferred_element_type=jnp.float32)
    up_part = jnp.dot(normed_two_low, w_up, preferred_element_type=jnp.float32)
    hidden_low = (jax.nn.silu(gate) * up_part).astype(jnp.bfloat16)
    output = mixed + jnp.dot(hidden_low, w_down, preferred_element_type=jnp.float32)
    kept = (
        states,
        scale_one,
        normed_low,
        query_low,
        window,
        log_total,
        attended_low,
        mixed,
        scale_two,
        normed_two_low,
        gate,
        up_part,
        hidden_low,
        cosine,
        sine,
        allowed,
    )
    return (output, kept)


def layer_backward(grad_output, kept, mats, gain_pair):
    w_query, w_key, w_value, w_out, w_gate, w_up, w_down = mats
    (
        states,
        scale_one,
        normed_low,
        query_low,
        window,
        log_total,
        attended_low,
        mixed,
        scale_two,
        normed_two_low,
        gate,
        up_part,
        hidden_low,
        cosine,
        sine,
        allowed,
    ) = kept
    rows = states.shape[0]
    group = HEADS // KV_HEADS
    kv_width = KV_HEADS * HEAD
    span = window.shape[0]
    grad_hidden = jnp.einsum("rd,fd->rf", grad_output, w_down, preferred_element_type=jnp.float32)
    sigmoid = jax.nn.sigmoid(gate)
    grad_gate = (grad_hidden * up_part * sigmoid * (1.0 + gate * (1.0 - sigmoid))).astype(
        jnp.bfloat16
    )
    grad_up = (grad_hidden * gate * sigmoid).astype(jnp.bfloat16)
    grad_normed_two = jnp.einsum("rf,df->rd", grad_gate, w_gate, preferred_element_type=jnp.float32)
    grad_normed_two = grad_normed_two + jnp.einsum(
        "rf,df->rd", grad_up, w_up, preferred_element_type=jnp.float32
    )
    grad_mixed = grad_output.astype(jnp.float32) + rms_back(
        mixed, scale_two, gain_pair[D:], grad_normed_two
    )
    grad_mixed_low = grad_mixed.astype(jnp.bfloat16)
    grad_attended = jnp.einsum(
        "rd,ed->re", grad_mixed_low, w_out, preferred_element_type=jnp.float32
    )
    grad_attended = grad_attended.astype(jnp.bfloat16).reshape(rows, KV_HEADS, group, HEAD)
    keys_win = window[:, :kv_width].reshape(span, KV_HEADS, HEAD)
    values_win = window[:, kv_width:].reshape(span, KV_HEADS, HEAD)
    grad_query, grad_keys, grad_values = attend_backward(
        query_low, keys_win, values_win, allowed, log_total, grad_attended
    )
    grad_window = jnp.concatenate(
        [grad_keys.reshape(span, kv_width), grad_values.reshape(span, kv_width)], axis=1
    )
    grad_pair = grad_window[REACH * rows :]
    for reach in range(1, REACH + 1):
        portion = grad_window[(REACH - reach) * rows : (REACH - reach + 1) * rows]
        grad_pair = grad_pair + passed_along(portion.astype(jnp.bfloat16), "fsdp", -reach).astype(
            portion.dtype
        )
    grad_key_low = rotate_back(grad_pair[:, :kv_width].reshape(rows, KV_HEADS, HEAD), cosine, sine)
    grad_key_low = grad_key_low.reshape(rows, kv_width).astype(jnp.bfloat16)
    grad_value_low = grad_pair[:, kv_width:].astype(jnp.bfloat16)
    grad_query_low = rotate_back(grad_query.reshape(rows, HEADS, HEAD), cosine, sine)
    grad_query_low = grad_query_low.reshape(rows, HEADS * HEAD).astype(jnp.bfloat16)
    grad_normed_one = jnp.einsum(
        "re,de->rd", grad_query_low, w_query, preferred_element_type=jnp.float32
    )
    grad_normed_one = grad_normed_one + jnp.einsum(
        "re,de->rd", grad_key_low, w_key, preferred_element_type=jnp.float32
    )
    grad_normed_one = grad_normed_one + jnp.einsum(
        "re,de->rd", grad_value_low, w_value, preferred_element_type=jnp.float32
    )
    grad_states = grad_mixed + rms_back(states, scale_one, gain_pair[:D], grad_normed_one)
    record = (
        normed_low,
        attended_low,
        normed_two_low,
        hidden_low,
        grad_query_low,
        grad_key_low,
        grad_value_low,
        grad_mixed_low,
        grad_gate,
        grad_up,
        grad_output,
        states * scale_one * grad_normed_one,
        mixed * scale_two * grad_normed_two,
    )
    return (grad_states, record)


def flat_terms(record):
    (
        normed_low,
        attended_low,
        normed_two_low,
        hidden_low,
        grad_query_low,
        grad_key_low,
        grad_value_low,
        grad_mixed_low,
        grad_gate,
        grad_up,
        grad_output,
        gain_term_one,
        gain_term_two,
    ) = record
    pieces = [
        jnp.einsum("rd,re->de", normed_low, grad_query_low, preferred_element_type=jnp.float32),
        jnp.einsum("rd,re->de", normed_low, grad_key_low, preferred_element_type=jnp.float32),
        jnp.einsum("rd,re->de", normed_low, grad_value_low, preferred_element_type=jnp.float32),
        jnp.einsum("re,rd->ed", attended_low, grad_mixed_low, preferred_element_type=jnp.float32),
        jnp.einsum("rd,rf->df", normed_two_low, grad_gate, preferred_element_type=jnp.float32),
        jnp.einsum("rd,rf->df", normed_two_low, grad_up, preferred_element_type=jnp.float32),
        jnp.einsum("rf,rd->fd", hidden_low, grad_output, preferred_element_type=jnp.float32),
    ]
    flat_grads = jnp.concatenate([piece.reshape(-1) for piece in pieces])
    gain_grad = jnp.concatenate([jnp.sum(gain_term_one, axis=0), jnp.sum(gain_term_two, axis=0)])
    return (flat_grads, gain_grad)


LANES = 128
SHARD_ROWS = 1728
GAIN_ROWS = 16
BLOCK_ROWS = SHARD_ROWS + GAIN_ROWS
PIECE_ROWS = 864
VMEM_LIMIT = 56 * 1024 * 1024


def lane_low(rows):
    return lax.broadcasted_iota(jnp.int32, (rows, LANES), 1) < 64


def swap_halves(value):
    return pltpu.roll(value, 64, 1)


def narrow_pack(wide, natural, out_ref, start, columns):
    full = columns // LANES
    period = 2 * full + 1
    pairs = PIECE_ROWS // period
    low = lane_low(pairs)
    part = [wide[pl.ds(start + j, pairs, stride=period), :] for j in range(period)]
    at = start
    for c in range(full):
        natural[pl.ds(0, pairs, stride=2), :] = part[c]
        natural[pl.ds(1, pairs, stride=2), :] = swap_halves(
            jnp.where(low, part[full + c + 1], part[full + c])
        )
        out_ref[at : at + 2 * pairs, :] = natural[0 : 2 * pairs, :].astype(jnp.bfloat16)
        at += 2 * pairs
    natural[pl.ds(0, pairs, stride=2), :] = part[full]
    natural[pl.ds(1, pairs, stride=2), :] = swap_halves(part[2 * full])
    out_ref[at : at + pairs, :] = jnp.where(
        low, natural[0:pairs, :], swap_halves(natural[pairs : 2 * pairs, :])
    ).astype(jnp.bfloat16)


def narrow_unpack(packed, natural, out_ref, start, columns):
    full = columns // LANES
    period = 2 * full + 1
    pairs = PIECE_ROWS // period
    low = lane_low(pairs)
    evens, odds = [], []
    at = start
    for c in range(full):
        natural[0 : 2 * pairs, :] = packed[at : at + 2 * pairs, :]
        evens.append(natural[pl.ds(0, pairs, stride=2), :])
        odds.append(swap_halves(natural[pl.ds(1, pairs, stride=2), :]))
        at += 2 * pairs
    tail = packed[at : at + pairs, :]
    natural[0:pairs, :] = tail
    natural[pairs : 2 * pairs, :] = swap_halves(tail)
    tail_even = natural[pl.ds(0, pairs, stride=2), :]
    tail_odd = swap_halves(natural[pl.ds(1, pairs, stride=2), :])
    rows = evens + [jnp.where(low, tail_even, odds[0])]
    for c in range(full - 1):
        rows.append(jnp.where(low, odds[c], odds[c + 1]))
    rows.append(jnp.where(low, odds[full - 1], tail_odd))
    for j in range(period):
        out_ref[pl.ds(start + j, pairs, stride=period), :] = rows[j]


def by_owner(owner, narrow, wide):
    @pl.when((owner == 0) | (owner == 3) | (owner >= 12))
    def _():
        narrow(0, D)
        narrow(PIECE_ROWS, D)

    @pl.when(owner == 1)
    def _():
        narrow(0, D)
        narrow(PIECE_ROWS, KV_HEADS * HEAD)

    @pl.when(owner == 2)
    def _():
        narrow(0, KV_HEADS * HEAD)
        narrow(PIECE_ROWS, D)

    @pl.when((owner >= 4) & (owner < 12))
    def _():
        wide()


def pack_kernel(owner_ref, flat_ref, gain_ref, out_ref, wide, natural):
    wide[...] = flat_ref[...].astype(jnp.float32)
    out_ref[SHARD_ROWS:BLOCK_ROWS, :] = gain_ref[...]

    def narrow(start, columns):
        narrow_pack(wide, natural, out_ref, start, columns)

    def broad():
        blocks = FF // LANES
        rows = SHARD_ROWS // blocks
        for c in range(blocks):
            out_ref[c * rows : (c + 1) * rows, :] = wide[pl.ds(c, rows, stride=blocks), :].astype(
                jnp.bfloat16
            )

    by_owner(owner_ref[0], narrow, broad)


def pack_shard(owner, flat, gain_rows):
    return pl.pallas_call(
        pack_kernel,
        out_shape=jax.ShapeDtypeStruct((BLOCK_ROWS, LANES), jnp.bfloat16),
        in_specs=[
            pl.BlockSpec(memory_space=pltpu.SMEM),
            pl.BlockSpec(memory_space=pltpu.VMEM),
            pl.BlockSpec(memory_space=pltpu.VMEM),
        ],
        out_specs=pl.BlockSpec(memory_space=pltpu.VMEM),
        scratch_shapes=[
            pltpu.VMEM((SHARD_ROWS, LANES), jnp.float32),
            pltpu.VMEM((1152, LANES), jnp.float32),
        ],
        compiler_params=pltpu.CompilerParams(vmem_limit_bytes=VMEM_LIMIT),
    )(owner, flat, gain_rows)


def finish_kernel(owner_ref, parts_ref, out_ref, gain_ref, total, natural):
    total[...] = jnp.sum(parts_ref[:, :SHARD_ROWS, :].astype(jnp.float32), axis=0)
    gain_ref[...] = jnp.sum(parts_ref[:, SHARD_ROWS:, :].astype(jnp.float32), axis=0)

    def narrow(start, columns):
        narrow_unpack(total, natural, out_ref, start, columns)

    def broad():
        blocks = FF // LANES
        rows = SHARD_ROWS // blocks
        for c in range(blocks):
            out_ref[pl.ds(c, rows, stride=blocks), :] = total[c * rows : (c + 1) * rows, :]

    by_owner(owner_ref[0], narrow, broad)


def finish_shard(owner, parts):
    return pl.pallas_call(
        finish_kernel,
        out_shape=(
            jax.ShapeDtypeStruct((SHARD_ROWS, LANES), jnp.float32),
            jax.ShapeDtypeStruct((GAIN_ROWS, LANES), jnp.float32),
        ),
        in_specs=[
            pl.BlockSpec(memory_space=pltpu.SMEM),
            pl.BlockSpec(memory_space=pltpu.VMEM),
        ],
        out_specs=(
            pl.BlockSpec(memory_space=pltpu.VMEM),
            pl.BlockSpec(memory_space=pltpu.VMEM),
        ),
        scratch_shapes=[
            pltpu.VMEM((SHARD_ROWS, LANES), jnp.float32),
            pltpu.VMEM((1152, LANES), jnp.float32),
        ],
        compiler_params=pltpu.CompilerParams(vmem_limit_bytes=VMEM_LIMIT),
    )(owner, parts)


def place_narrow(block, at, target, row, columns):
    full = columns // LANES
    pairs = PIECE_ROWS // (2 * full + 1)
    for c in range(full):
        target[pl.ds(row, 2 * pairs), c * LANES : (c + 1) * LANES] = block[at : at + 2 * pairs, :]
        at += 2 * pairs
    target[pl.ds(row, pairs), full * LANES :] = block[at : at + pairs, :64]
    target[pl.ds(row + pairs, pairs), full * LANES :] = block[at : at + pairs, 64:]


def place_kernel(owners_ref, block_ref, query, key, value, out, gate, up, down):
    owner = owners_ref[pl.program_id(0)]
    block = block_ref.at[0]
    kv_width = KV_HEADS * HEAD

    @pl.when(owner == 0)
    def _():
        place_narrow(block, 0, query, 0, D)
        place_narrow(block, PIECE_ROWS, query, 192, D)

    @pl.when(owner == 1)
    def _():
        place_narrow(block, 0, query, 384, D)
        place_narrow(block, PIECE_ROWS, key, 0, kv_width)

    @pl.when(owner == 2)
    def _():
        place_narrow(block, 0, value, 0, kv_width)
        place_narrow(block, PIECE_ROWS, out, 0, D)

    @pl.when(owner == 3)
    def _():
        place_narrow(block, 0, out, 192, D)
        place_narrow(block, PIECE_ROWS, out, 384, D)

    def broad(target, first):
        @pl.when((owner >= first) & (owner < first + 4))
        def _():
            row = pl.multiple_of((owner - first) * 144, 16)
            for c in range(FF // LANES):
                target[pl.ds(row, 144), c * LANES : (c + 1) * LANES] = block[
                    c * 144 : (c + 1) * 144, :
                ]

    broad(gate, 4)
    broad(up, 8)

    @pl.when(owner >= 12)
    def _():
        row = pl.multiple_of((owner - 12) * 384, 16)
        place_narrow(block, 0, down, row, D)
        place_narrow(block, PIECE_ROWS, down, pl.multiple_of(row + 192, 16), D)


def place_blocks(owners, blocks):
    kv_width = KV_HEADS * HEAD
    shapes = [(D, D), (D, kv_width), (D, kv_width), (D, D), (D, FF), (D, FF), (FF, D)]
    return pl.pallas_call(
        place_kernel,
        out_shape=tuple(jax.ShapeDtypeStruct(shape, jnp.bfloat16) for shape in shapes),
        grid_spec=pltpu.PrefetchScalarGridSpec(
            num_scalar_prefetch=1,
            grid=(16,),
            in_specs=[pl.BlockSpec((1, BLOCK_ROWS, LANES), lambda r, owners: (r, 0, 0))],
            out_specs=tuple(pl.BlockSpec(shape, lambda r, owners: (0, 0)) for shape in shapes),
        ),
        compiler_params=pltpu.CompilerParams(vmem_limit_bytes=VMEM_LIMIT),
    )(owners, blocks)


def store_narrow(result, block, at, columns):
    full = columns // LANES
    pairs = PIECE_ROWS // (2 * full + 1)
    result = result.astype(jnp.bfloat16)
    for c in range(full):
        block[at : at + 2 * pairs, :] = result[:, c * LANES : (c + 1) * LANES]
        at += 2 * pairs
    block[at : at + pairs, :] = jnp.concatenate(
        [result[:pairs, full * LANES :], result[pairs:, full * LANES :]], axis=1
    )


def terms_kernel(
    owners_ref,
    normed,
    attended,
    normed_two,
    hidden,
    grad_query,
    grad_key,
    grad_value,
    grad_mixed,
    grad_gate,
    grad_up,
    grad_output,
    gain_ref,
    out_ref,
    normed_t,
    attended_t,
    normed_two_t,
    hidden_t,
):
    owner = owners_ref[pl.program_id(0)]
    block = out_ref.at[0]
    kv_width = KV_HEADS * HEAD

    @pl.when(pl.program_id(0) == 0)
    def _():
        for whole, turned in (
            (normed, normed_t),
            (attended, attended_t),
            (normed_two, normed_two_t),
            (hidden, hidden_t),
        ):
            turned[...] = whole[...].T

    block[SHARD_ROWS:BLOCK_ROWS, :] = gain_ref[0]

    def product(turned, row, count, right):
        return jnp.dot(turned[pl.ds(row, count), :], right[...], preferred_element_type=jnp.float32)

    @pl.when(owner == 0)
    def _():
        store_narrow(product(normed_t, 0, 192, grad_query), block, 0, D)
        store_narrow(product(normed_t, 192, 192, grad_query), block, PIECE_ROWS, D)

    @pl.when(owner == 1)
    def _():
        store_narrow(product(normed_t, 384, 192, grad_query), block, 0, D)
        store_narrow(product(normed_t, 0, D, grad_key), block, PIECE_ROWS, kv_width)

    @pl.when(owner == 2)
    def _():
        store_narrow(product(normed_t, 0, D, grad_value), block, 0, kv_width)
        store_narrow(product(attended_t, 0, 192, grad_mixed), block, PIECE_ROWS, D)

    @pl.when(owner == 3)
    def _():
        store_narrow(product(attended_t, 192, 192, grad_mixed), block, 0, D)
        store_narrow(product(attended_t, 384, 192, grad_mixed), block, PIECE_ROWS, D)

    def broad(right, first):
        @pl.when((owner >= first) & (owner < first + 4))
        def _():
            row = pl.multiple_of((owner - first) * 144, 16)
            result = product(normed_two_t, row, 144, right).astype(jnp.bfloat16)
            for c in range(FF // LANES):
                block[c * 144 : (c + 1) * 144, :] = result[:, c * LANES : (c + 1) * LANES]

    broad(grad_gate, 4)
    broad(grad_up, 8)

    @pl.when(owner >= 12)
    def _():
        row = pl.multiple_of((owner - 12) * 384, 16)
        store_narrow(product(hidden_t, row, 192, grad_output), block, 0, D)
        store_narrow(
            product(hidden_t, pl.multiple_of(row + 192, 16), 192, grad_output), block, PIECE_ROWS, D
        )


def terms_blocks(owners, factors, gain_rows):
    rows = factors[0].shape[0]

    def whole(shape):
        return pl.BlockSpec(shape, lambda r, owners: (0,) * len(shape))

    return pl.pallas_call(
        terms_kernel,
        out_shape=jax.ShapeDtypeStruct((16, BLOCK_ROWS, LANES), jnp.bfloat16),
        grid_spec=pltpu.PrefetchScalarGridSpec(
            num_scalar_prefetch=1,
            grid=(16,),
            in_specs=[whole(item.shape) for item in factors]
            + [pl.BlockSpec((1, GAIN_ROWS, LANES), lambda r, owners: (owners[r], 0, 0))],
            out_specs=pl.BlockSpec((1, BLOCK_ROWS, LANES), lambda r, owners: (r, 0, 0)),
            scratch_shapes=[
                pltpu.VMEM((D, rows), jnp.bfloat16),
                pltpu.VMEM((D, rows), jnp.bfloat16),
                pltpu.VMEM((D, rows), jnp.bfloat16),
                pltpu.VMEM((FF, rows), jnp.bfloat16),
            ],
        ),
        compiler_params=pltpu.CompilerParams(vmem_limit_bytes=VMEM_LIMIT),
    )(owners, *factors, gain_rows)


def gather_layer(weights, gains):
    owners = lax.axis_size("fsdp")
    if owners != 16:
        flat_full = lax.all_gather(weights[0], "fsdp", axis=0, tiled=True)
        gain_full = lax.all_gather(gains[0], "fsdp", axis=0, tiled=True)
        return unpack(flat_full), gain_full.astype(jnp.float32)
    owner = lax.axis_index("fsdp").astype(jnp.int32).reshape(1)
    share = gains.shape[1]
    gain_rows = jnp.pad(gains, ((0, GAIN_ROWS - 1), (0, LANES - share)))
    packed = pack_shard(owner, weights.reshape(SHARD_ROWS, LANES), gain_rows)
    blocks = lax.all_gather(packed, "fsdp", axis=0, tiled=True).reshape(16, BLOCK_ROWS, LANES)
    mats = place_blocks(jnp.arange(16, dtype=jnp.int32), blocks)
    gain_full = blocks[:, SHARD_ROWS, :share].reshape(-1)
    return mats, gain_full.astype(jnp.float32)


def reduce_terms(joined):
    owners = lax.axis_size("fsdp")
    if owners != 16:
        flat_grads, gain_grad = flat_terms(joined)
        got = [
            lax.all_to_all(
                item.reshape(owners, -1).astype(jnp.bfloat16),
                "fsdp",
                split_axis=0,
                concat_axis=0,
                tiled=True,
            ).astype(jnp.float32)
            for item in (flat_grads, gain_grad)
        ]
        return tuple(jnp.sum(item, axis=0) for item in got)
    gain_grad = jnp.concatenate([jnp.sum(joined[11], axis=0), jnp.sum(joined[12], axis=0)])
    share = gain_grad.shape[0] // owners
    gain_rows = jnp.pad(
        gain_grad.reshape(owners, 1, share).astype(jnp.bfloat16),
        ((0, 0), (0, GAIN_ROWS - 1), (0, LANES - share)),
    )
    blocks = terms_blocks(jnp.arange(16, dtype=jnp.int32), joined[:11], gain_rows)
    parts = lax.all_to_all(blocks, "fsdp", split_axis=0, concat_axis=0, tiled=True)
    owner = lax.axis_index("fsdp").astype(jnp.int32).reshape(1)
    flat, gain = finish_shard(owner, parts)
    return flat.reshape(-1), gain[0, :share]


def local(ends, weights, gains, segments):
    micro_count = ends.shape[1]
    rows = ends.shape[2]
    owners = lax.axis_size("fsdp")
    first = lax.axis_index("section") == 0
    marked = segments + 1
    rims = [marked]
    for reach in range(1, REACH + 1):
        rims.insert(0, passed_along(marked, "fsdp", reach))
    window_segments = jnp.concatenate(rims, axis=1)
    span = window_segments.shape[1]
    place = jnp.arange(span, dtype=jnp.int32)
    change = jnp.concatenate(
        [jnp.ones((micro_count, 1), dtype=bool), window_segments[:, 1:] != window_segments[:, :-1]],
        axis=1,
    )
    starts = lax.cummax(jnp.where(change, place[None, :], 0), axis=1)
    positions = (place[None, :] - starts)[:, span - rows :]
    own_segments = window_segments[:, span - rows :]
    query_place = place[span - rows :]
    tables = []
    for micro in range(micro_count):
        cosine, sine = rope_tables(positions[micro])
        allowed = (own_segments[micro][:, None] == window_segments[micro][None, :]) & (
            place[None, :] <= query_place[:, None]
        )
        tables.append((cosine, sine, allowed))
    mats, gain_pair = gather_layer(weights, gains)
    own_inputs = ends[0]
    nothing = jnp.zeros_like(own_inputs[0])
    received = nothing
    kept_steps = []
    outputs = []
    for step in range(micro_count + 1):
        mine = own_inputs[step] if step < micro_count else nothing
        states = jnp.where(first, mine, received).astype(jnp.float32)
        table = select(first, tables[min(step, micro_count - 1)], tables[max(step - 1, 0)])
        output, kept = layer_forward(states, mats, gain_pair, table)
        kept_steps.append(kept)
        outputs.append(output)
        if step < micro_count:
            received = passed_along(output.astype(jnp.bfloat16), "section", 1)
    back_mats, back_gains = mats, gain_pair
    coming = nothing
    grad_inputs = []
    records = []
    for step in range(micro_count + 1):
        mine = own_inputs[step] if step < micro_count else nothing
        grad_output = jnp.where(first, coming, mine)
        kept = select(first, kept_steps[max(step - 1, 0)], kept_steps[min(step + 1, micro_count)])
        grad_states, record = layer_backward(grad_output, kept, back_mats, back_gains)
        grad_inputs.append(grad_states)
        records.append(record)
        if step < micro_count:
            coming = passed_along(grad_states.astype(jnp.bfloat16), "section", -1)
    chosen = [select(first, records[micro + 1], records[micro]) for micro in range(micro_count)]
    joined = tuple(
        (
            jnp.concatenate([item[number] for item in chosen], axis=0)
            for number in range(len(chosen[0]))
        )
    )
    weight_share, gain_share = reduce_terms(joined)
    ends_out = jnp.stack(
        [
            jnp.where(first, grad_inputs[micro + 1], outputs[micro + 1])
            for micro in range(micro_count)
        ]
    )
    return (ends_out.astype(jnp.bfloat16)[None], weight_share[None], gain_share[None])


def solution(mesh):
    placed = (
        P("section", None, "fsdp", None),
        P("section", "fsdp"),
        P("section", "fsdp"),
        P(None, "fsdp"),
    )
    return jax.shard_map(
        local,
        mesh=mesh,
        in_specs=placed,
        out_specs=(P("section", None, "fsdp", None), P("section", "fsdp"), P("section", "fsdp")),
        check_vma=False,
    )
```

```python
import jax
import jax.numpy as jnp
from jax import lax
from jax.experimental import pallas as pl
from jax.experimental.pallas import tpu as pltpu
from jax.sharding import PartitionSpec as P

D = 576
HEADS = 9
KV_HEADS = 3
HEAD = 64
FF = 1536
REACH = 2


epsilon = 1e-05
rope_base = 100000.0
masked_score = -1e30


def passed_along(value, axis, steps):
    count = lax.axis_size(axis)
    first, last = (max(0, -steps), min(count, count - steps))
    return lax.ppermute(value, axis, [(source, source + steps) for source in range(first, last)])


def rope_tables(positions):
    half = HEAD // 2
    frequency = rope_base ** (-2.0 * jnp.arange(half, dtype=jnp.float32) / HEAD)
    angles = positions.astype(jnp.float32)[:, None] * frequency[None, :]
    return (jnp.cos(angles), jnp.sin(angles))


def rms_scale(states):
    return lax.rsqrt(jnp.mean(states * states, axis=-1, keepdims=True) + epsilon)


def rms_back(states, scale, gain, grad):
    weighted = grad * gain
    return scale * weighted - states * (scale * scale * scale) * jnp.mean(
        weighted * states, axis=-1, keepdims=True
    )


def unpack(flat_vector):
    query_cols = HEADS * HEAD
    kv_cols = KV_HEADS * HEAD
    shapes = [
        (D, query_cols),
        (D, kv_cols),
        (D, kv_cols),
        (query_cols, D),
        (D, FF),
        (D, FF),
        (FF, D),
    ]
    pieces = []
    offset = 0
    for row_count, col_count in shapes:
        pieces.append(
            flat_vector[offset : offset + row_count * col_count].reshape(row_count, col_count)
        )
        offset = offset + row_count * col_count
    return pieces


LANES = 128
SHARD_ROWS = 1728
GAIN_ROWS = 16
BLOCK_ROWS = SHARD_ROWS + GAIN_ROWS
PIECE_ROWS = 864
VMEM_LIMIT = 56 * 1024 * 1024


def lane_low(rows):
    return lax.broadcasted_iota(jnp.int32, (rows, LANES), 1) < 64


def swap_halves(value):
    return pltpu.roll(value, 64, 1)


def narrow_pack(wide, natural, out_ref, start, columns):
    full = columns // LANES
    period = 2 * full + 1
    pairs = PIECE_ROWS // period
    low = lane_low(pairs)
    part = [wide[pl.ds(start + j, pairs, stride=period), :] for j in range(period)]
    at = start
    for c in range(full):
        natural[pl.ds(0, pairs, stride=2), :] = part[c]
        natural[pl.ds(1, pairs, stride=2), :] = swap_halves(
            jnp.where(low, part[full + c + 1], part[full + c])
        )
        out_ref[at : at + 2 * pairs, :] = natural[0 : 2 * pairs, :].astype(jnp.bfloat16)
        at += 2 * pairs
    natural[pl.ds(0, pairs, stride=2), :] = part[full]
    natural[pl.ds(1, pairs, stride=2), :] = swap_halves(part[2 * full])
    out_ref[at : at + pairs, :] = jnp.where(
        low, natural[0:pairs, :], swap_halves(natural[pairs : 2 * pairs, :])
    ).astype(jnp.bfloat16)


def narrow_unpack(packed, natural, out_ref, start, columns):
    full = columns // LANES
    period = 2 * full + 1
    pairs = PIECE_ROWS // period
    low = lane_low(pairs)
    evens, odds = [], []
    at = start
    for c in range(full):
        natural[0 : 2 * pairs, :] = packed[at : at + 2 * pairs, :]
        evens.append(natural[pl.ds(0, pairs, stride=2), :])
        odds.append(swap_halves(natural[pl.ds(1, pairs, stride=2), :]))
        at += 2 * pairs
    tail = packed[at : at + pairs, :]
    natural[0:pairs, :] = tail
    natural[pairs : 2 * pairs, :] = swap_halves(tail)
    tail_even = natural[pl.ds(0, pairs, stride=2), :]
    tail_odd = swap_halves(natural[pl.ds(1, pairs, stride=2), :])
    rows = evens + [jnp.where(low, tail_even, odds[0])]
    for c in range(full - 1):
        rows.append(jnp.where(low, odds[c], odds[c + 1]))
    rows.append(jnp.where(low, odds[full - 1], tail_odd))
    for j in range(period):
        out_ref[pl.ds(start + j, pairs, stride=period), :] = rows[j]


def by_owner(owner, narrow, wide):
    @pl.when((owner == 0) | (owner == 3) | (owner >= 12))
    def _():
        narrow(0, D)
        narrow(PIECE_ROWS, D)

    @pl.when(owner == 1)
    def _():
        narrow(0, D)
        narrow(PIECE_ROWS, KV_HEADS * HEAD)

    @pl.when(owner == 2)
    def _():
        narrow(0, KV_HEADS * HEAD)
        narrow(PIECE_ROWS, D)

    @pl.when((owner >= 4) & (owner < 12))
    def _():
        wide()


def pack_kernel(owner_ref, flat_ref, gain_ref, out_ref, wide, natural):
    wide[...] = flat_ref[...].astype(jnp.float32)
    out_ref[SHARD_ROWS:BLOCK_ROWS, :] = gain_ref[...]

    def narrow(start, columns):
        narrow_pack(wide, natural, out_ref, start, columns)

    def broad():
        blocks = FF // LANES
        rows = SHARD_ROWS // blocks
        for c in range(blocks):
            out_ref[c * rows : (c + 1) * rows, :] = wide[pl.ds(c, rows, stride=blocks), :].astype(
                jnp.bfloat16
            )

    by_owner(owner_ref[0], narrow, broad)


def pack_shard(owner, flat, gain_rows):
    return pl.pallas_call(
        pack_kernel,
        out_shape=jax.ShapeDtypeStruct((BLOCK_ROWS, LANES), jnp.bfloat16),
        in_specs=[
            pl.BlockSpec(memory_space=pltpu.SMEM),
            pl.BlockSpec(memory_space=pltpu.VMEM),
            pl.BlockSpec(memory_space=pltpu.VMEM),
        ],
        out_specs=pl.BlockSpec(memory_space=pltpu.VMEM),
        scratch_shapes=[
            pltpu.VMEM((SHARD_ROWS, LANES), jnp.float32),
            pltpu.VMEM((1152, LANES), jnp.float32),
        ],
        compiler_params=pltpu.CompilerParams(vmem_limit_bytes=VMEM_LIMIT),
    )(owner, flat, gain_rows)


def finish_kernel(owner_ref, *refs):
    count = len(REDUCE_CUTS) - 1
    kept_refs, got_refs = refs[:count], refs[count : 2 * count]
    out_ref, gain_ref, total, natural = refs[2 * count :]
    for number in range(count):
        total[REDUCE_CUTS[number] : REDUCE_CUTS[number + 1], :] = kept_refs[number][
            ...
        ].astype(jnp.float32) + got_refs[number][...].astype(jnp.float32)
    gain_ref[...] = total[SHARD_ROWS:, :]

    def narrow(start, columns):
        narrow_unpack(total, natural, out_ref, start, columns)

    def broad():
        blocks = FF // LANES
        rows = SHARD_ROWS // blocks
        for c in range(blocks):
            out_ref[pl.ds(c, rows, stride=blocks), :] = total[c * rows : (c + 1) * rows, :]

    by_owner(owner_ref[0], narrow, broad)


def in_vmem(count):
    return [pl.BlockSpec(memory_space=pltpu.VMEM)] * count


def finish_shard(owner, kept, got):
    return pl.pallas_call(
        finish_kernel,
        out_shape=(
            jax.ShapeDtypeStruct((SHARD_ROWS, LANES), jnp.float32),
            jax.ShapeDtypeStruct((GAIN_ROWS, LANES), jnp.float32),
        ),
        in_specs=[pl.BlockSpec(memory_space=pltpu.SMEM)] + in_vmem(len(kept) + len(got)),
        out_specs=tuple(in_vmem(2)),
        scratch_shapes=[
            pltpu.VMEM((BLOCK_ROWS, LANES), jnp.float32),
            pltpu.VMEM((1152, LANES), jnp.float32),
        ],
        compiler_params=pltpu.CompilerParams(vmem_limit_bytes=VMEM_LIMIT),
    )(owner, *kept, *got)


SLOTS = 1024
KEY_MAIN = 640
KEY_TAIL = 576
VALUE_MAIN = 768
VALUE_TAIL = 896
GATHER_CUTS = (0, 544, 1088, 1408, 1744)
GATHER_ORDERS = ((8, 4, 2, 1), (4, 8, 1, 2), (2, 1, 8, 4), (1, 2, 4, 8))
REDUCE_CUTS = (0, 608, 1216, 1744)
REDUCE_ORDERS = ((1, 2, 4, 8), (2, 1, 8, 4), (4, 8, 1, 2))


def place_narrow(block, at, target, row, main, tail, columns):
    full = columns // LANES
    pairs = PIECE_ROWS // (2 * full + 1)
    for c in range(full):
        target[pl.ds(row, 2 * pairs), main + c * LANES : main + (c + 1) * LANES] = block[
            at : at + 2 * pairs, :
        ]
        at += 2 * pairs
    target[pl.ds(row, pairs), tail : tail + 64] = block[at : at + pairs, :64]
    target[pl.ds(row + pairs, pairs), tail : tail + 64] = block[at : at + pairs, 64:]


def place_kernel(index_ref, *refs):
    count = len(GATHER_CUTS) - 1
    chunks = refs[:count]
    joined, out, gate, up, down, gain, block = refs[count:]
    owner = pl.program_id(0)
    kv_width = KV_HEADS * HEAD
    for number in range(count):
        block[GATHER_CUTS[number] : GATHER_CUTS[number + 1], :] = chunks[number][0]
    gain[...] = block[SHARD_ROWS:, :]

    @pl.when(owner == 0)
    def _():
        joined[:, SLOTS - 128 :] = jnp.zeros((D, 128), jnp.bfloat16)
        place_narrow(block, 0, joined, 0, 0, 512, D)
        place_narrow(block, PIECE_ROWS, joined, 192, 0, 512, D)

    @pl.when(owner == 1)
    def _():
        place_narrow(block, 0, joined, 384, 0, 512, D)
        place_narrow(block, PIECE_ROWS, joined, 0, KEY_MAIN, KEY_TAIL, kv_width)

    @pl.when(owner == 2)
    def _():
        place_narrow(block, 0, joined, 0, VALUE_MAIN, VALUE_TAIL, kv_width)
        place_narrow(block, PIECE_ROWS, out, 0, 0, 512, D)

    @pl.when(owner == 3)
    def _():
        place_narrow(block, 0, out, 192, 0, 512, D)
        place_narrow(block, PIECE_ROWS, out, 384, 0, 512, D)

    def broad(target, first):
        @pl.when((owner >= first) & (owner < first + 4))
        def _():
            row = pl.multiple_of((owner - first) * 144, 16)
            for c in range(FF // LANES):
                target[pl.ds(row, 144), c * LANES : (c + 1) * LANES] = block[
                    c * 144 : (c + 1) * 144, :
                ]

    broad(gate, 4)
    broad(up, 8)

    @pl.when(owner >= 12)
    def _():
        row = pl.multiple_of((owner - 12) * 384, 16)
        place_narrow(block, 0, down, row, 0, 512, D)
        place_narrow(block, PIECE_ROWS, down, pl.multiple_of(row + 192, 16), 0, 512, D)


def chunk_spec(cuts, number):
    return pl.BlockSpec(
        (1, cuts[number + 1] - cuts[number], LANES),
        lambda s, index: (index[number, s], 0, 0),
    )


def place_blocks(index, chunks):
    shapes = [(D, SLOTS), (D, D), (D, FF), (D, FF), (FF, D)]
    return pl.pallas_call(
        place_kernel,
        out_shape=tuple(jax.ShapeDtypeStruct(shape, jnp.bfloat16) for shape in shapes)
        + (jax.ShapeDtypeStruct((16 * GAIN_ROWS, LANES), jnp.bfloat16),),
        grid_spec=pltpu.PrefetchScalarGridSpec(
            num_scalar_prefetch=1,
            grid=(16,),
            in_specs=[chunk_spec(GATHER_CUTS, number) for number in range(len(chunks))],
            out_specs=tuple(pl.BlockSpec(shape, lambda s, index: (0, 0)) for shape in shapes)
            + (pl.BlockSpec((GAIN_ROWS, LANES), lambda s, index: (s, 0)),),
            scratch_shapes=[pltpu.VMEM((BLOCK_ROWS, LANES), jnp.bfloat16)],
        ),
        compiler_params=pltpu.CompilerParams(vmem_limit_bytes=VMEM_LIMIT),
    )(index, *chunks)


def store_narrow(result, block, at, main, tail, columns):
    full = columns // LANES
    pairs = PIECE_ROWS // (2 * full + 1)
    for c in range(full):
        block[at : at + 2 * pairs, :] = result[
            :, main + c * LANES : main + (c + 1) * LANES
        ].astype(jnp.bfloat16)
        at += 2 * pairs
    block[at : at + pairs, :] = jnp.concatenate(
        [result[:pairs, tail : tail + 64], result[pairs:, tail : tail + 64]], axis=1
    ).astype(jnp.bfloat16)


def terms_kernel(
    index_ref,
    normed,
    attended,
    normed_two,
    hidden,
    grad_joined,
    grad_mixed,
    grad_gate,
    grad_up,
    grad_output,
    gain_ref,
    *refs,
):
    count = len(REDUCE_CUTS) - 1
    chunks = refs[:count]
    block, normed_t, attended_t, normed_two_t, hidden_t = refs[count:]
    owner = pl.program_id(0)
    kv_width = KV_HEADS * HEAD

    @pl.when(owner == 0)
    def _():
        for whole, turned in (
            (normed, normed_t),
            (attended, attended_t),
            (normed_two, normed_two_t),
            (hidden, hidden_t),
        ):
            turned[...] = whole[...].T

    block[SHARD_ROWS:BLOCK_ROWS, :] = gain_ref[0]

    def product(turned, row, count, right):
        return jnp.dot(turned[pl.ds(row, count), :], right, preferred_element_type=jnp.float32)

    @pl.when(owner == 0)
    def _():
        query = grad_joined[:, :KEY_MAIN]
        store_narrow(product(normed_t, 0, 192, query), block, 0, 0, 512, D)
        store_narrow(product(normed_t, 192, 192, query), block, PIECE_ROWS, 0, 512, D)

    @pl.when(owner == 1)
    def _():
        store_narrow(
            product(normed_t, 384, 192, grad_joined[:, :KEY_MAIN]), block, 0, 0, 512, D
        )
        key = product(normed_t, 0, D, grad_joined[:, 512:768])
        store_narrow(key, block, PIECE_ROWS, KEY_MAIN - 512, KEY_TAIL - 512, kv_width)

    @pl.when(owner == 2)
    def _():
        value = product(normed_t, 0, D, grad_joined[:, VALUE_MAIN:])
        store_narrow(value, block, 0, 0, VALUE_TAIL - VALUE_MAIN, kv_width)
        store_narrow(
            product(attended_t, 0, 192, grad_mixed[...]), block, PIECE_ROWS, 0, 512, D
        )

    @pl.when(owner == 3)
    def _():
        store_narrow(product(attended_t, 192, 192, grad_mixed[...]), block, 0, 0, 512, D)
        store_narrow(
            product(attended_t, 384, 192, grad_mixed[...]), block, PIECE_ROWS, 0, 512, D
        )

    def broad(right, first):
        @pl.when((owner >= first) & (owner < first + 4))
        def _():
            row = pl.multiple_of((owner - first) * 144, 16)
            result = product(normed_two_t, row, 144, right[...]).astype(jnp.bfloat16)
            for c in range(FF // LANES):
                block[c * 144 : (c + 1) * 144, :] = result[:, c * LANES : (c + 1) * LANES]

    broad(grad_gate, 4)
    broad(grad_up, 8)

    @pl.when(owner >= 12)
    def _():
        for half in range(2):
            row = pl.multiple_of((owner - 12) * 384 + half * 192, 16)
            store_narrow(
                product(hidden_t, row, 192, grad_output[...]), block, half * PIECE_ROWS, 0, 512, D
            )

    for number in range(count):
        chunks[number][0] = block[REDUCE_CUTS[number] : REDUCE_CUTS[number + 1], :]


def terms_blocks(index, factors, gain_rows):
    rows = factors[0].shape[0]
    count = len(REDUCE_CUTS) - 1

    def whole(shape):
        return pl.BlockSpec(shape, lambda s, index: (0,) * len(shape))

    return pl.pallas_call(
        terms_kernel,
        out_shape=tuple(
            jax.ShapeDtypeStruct(
                (16, REDUCE_CUTS[number + 1] - REDUCE_CUTS[number], LANES), jnp.bfloat16
            )
            for number in range(count)
        ),
        grid_spec=pltpu.PrefetchScalarGridSpec(
            num_scalar_prefetch=1,
            grid=(16,),
            in_specs=[whole(item.shape) for item in factors]
            + [pl.BlockSpec((1, GAIN_ROWS, LANES), lambda s, index: (s, 0, 0))],
            out_specs=tuple(chunk_spec(REDUCE_CUTS, number) for number in range(count)),
            scratch_shapes=[
                pltpu.VMEM((BLOCK_ROWS, LANES), jnp.bfloat16),
                pltpu.VMEM((D, rows), jnp.bfloat16),
                pltpu.VMEM((D, rows), jnp.bfloat16),
                pltpu.VMEM((D, rows), jnp.bfloat16),
                pltpu.VMEM((FF, rows), jnp.bfloat16),
            ],
        ),
        compiler_params=pltpu.CompilerParams(vmem_limit_bytes=VMEM_LIMIT),
    )(index, *factors, gain_rows)


def partner(value, stride):
    count = lax.axis_size("fsdp")
    return lax.ppermute(value, "fsdp", [(source, source ^ stride) for source in range(count)])


def block_index(orders, first_is_low):
    apart = jnp.arange(16, dtype=jnp.int32) ^ lax.axis_index("fsdp").astype(jnp.int32)
    rows = []
    for order in orders:
        place = jnp.zeros_like(apart)
        for stage, stride in enumerate(order):
            bit = stage if first_is_low else len(order) - 1 - stage
            place = place + jnp.where((apart & stride) != 0, 1 << bit, 0)
        rows.append(place)
    return jnp.stack(rows)


def gather_layer(weights, gains):
    owners = lax.axis_size("fsdp")
    if owners != 16:
        flat_full = lax.all_gather(weights[0], "fsdp", axis=0, tiled=True)
        gain_full = lax.all_gather(gains[0], "fsdp", axis=0, tiled=True)
        query, key, value, out, gate, up, down = unpack(flat_full)
        joined = jnp.concatenate(
            [
                query,
                key[:, LANES:],
                key[:, :LANES],
                value,
                jnp.zeros((D, SLOTS - VALUE_TAIL - 64), jnp.bfloat16),
            ],
            axis=1,
        )
        return (joined, out, gate, up, down), gain_full.astype(jnp.float32).reshape(2, D)
    owner = lax.axis_index("fsdp").astype(jnp.int32).reshape(1)
    share = gains.shape[1]
    gain_rows = jnp.pad(gains, ((0, GAIN_ROWS - 1), (0, LANES - share)))
    packed = pack_shard(owner, weights.reshape(SHARD_ROWS, LANES), gain_rows)
    chunks = [
        packed[GATHER_CUTS[number] : GATHER_CUTS[number + 1]]
        for number in range(len(GATHER_ORDERS))
    ]
    for stage in range(4):
        got = [partner(chunk, order[stage]) for chunk, order in zip(chunks, GATHER_ORDERS)]
        chunks = [jnp.concatenate(both) for both in zip(chunks, got)]
    chunks = [chunk.reshape(16, -1, LANES) for chunk in chunks]
    *mats, gain_full = place_blocks(block_index(GATHER_ORDERS, True), chunks)
    gain_full = gain_full.reshape(16, GAIN_ROWS, LANES)[:, 0, :share]
    return tuple(mats), gain_full.astype(jnp.float32).reshape(2, D)


def reduce_terms(factors, gain_grad):
    owners = lax.axis_size("fsdp")
    share = gain_grad.shape[0] // owners
    if owners != 16:
        normed, attended, normed_two, hidden, joined, grad_mixed, grad_gate, grad_up, last = factors
        pairs = [
            (normed, joined[:, :D]),
            (normed, jnp.concatenate([joined[:, KEY_MAIN:VALUE_MAIN], joined[:, D:KEY_MAIN]], 1)),
            (normed, joined[:, VALUE_MAIN : VALUE_TAIL + 64]),
            (attended, grad_mixed),
            (normed_two, grad_gate),
            (normed_two, grad_up),
            (hidden, last),
        ]
        flat_grads = jnp.concatenate(
            [
                jnp.einsum("rd,re->de", left, right, preferred_element_type=jnp.float32).reshape(-1)
                for left, right in pairs
            ]
        )
        got = [
            lax.all_to_all(
                item.reshape(owners, -1).astype(jnp.bfloat16),
                "fsdp",
                split_axis=0,
                concat_axis=0,
                tiled=True,
            ).astype(jnp.float32)
            for item in (flat_grads, gain_grad)
        ]
        return tuple(jnp.sum(item, axis=0) for item in got)
    gain_rows = jnp.pad(
        gain_grad.reshape(owners, 1, share).astype(jnp.bfloat16),
        ((0, 0), (0, GAIN_ROWS - 1), (0, LANES - share)),
    )
    sums = terms_blocks(block_index(REDUCE_ORDERS, False), factors, gain_rows)
    for stage in range(4):
        half = 8 >> stage
        got = [partner(item[half:], order[stage]) for item, order in zip(sums, REDUCE_ORDERS)]
        kept = [item[:half] for item in sums]
        if stage < 3:
            sums = [
                (one.astype(jnp.float32) + other.astype(jnp.float32)).astype(jnp.bfloat16)
                for one, other in zip(kept, got)
            ]
    owner = lax.axis_index("fsdp").astype(jnp.int32).reshape(1)
    flat, gain = finish_shard(owner, [item[0] for item in kept], [item[0] for item in got])
    return flat.reshape(-1), gain[0, :share]


def turned(block, cosine, sine):
    low = lax.broadcasted_iota(jnp.int32, block.shape, 1) % 64 < 32
    other = jnp.where(low, pltpu.roll(block, 96, 1), pltpu.roll(block, 32, 1))
    return block * cosine + other * sine


def lanes(value, number):
    return value[:, number * LANES : (number + 1) * LANES]


def project_kernel(states_ref, gain, joined, cosine, sine, normed, query, pair):
    states = states_ref[...].astype(jnp.float32)
    low_rows = (states * rms_scale(states) * gain[0:1, :]).astype(jnp.bfloat16)
    normed[...] = low_rows
    full = jnp.dot(low_rows, joined[...], preferred_element_type=jnp.float32)
    blocks = [turned(lanes(full, number), cosine[...], sine[...]) for number in range(6)]
    for number in range(5):
        query[:, number * LANES : (number + 1) * LANES] = blocks[number].astype(jnp.bfloat16)
    low = lane_low(full.shape[0])
    pair[:, :LANES] = blocks[5].astype(jnp.bfloat16)
    pair[:, LANES : 2 * LANES] = lanes(full, 6).astype(jnp.bfloat16)
    pair[:, 2 * LANES :] = jnp.where(
        low, swap_halves(blocks[4]), swap_halves(lanes(full, 7))
    ).astype(jnp.bfloat16)


KEY_AT = (0, 64, 256)
VALUE_AT = (128, 192, 320)


def fill_window(window, pieces):
    micro_count, span, _ = window.shape
    rows = span // len(pieces)
    for micro in range(micro_count):
        for number, piece in enumerate(pieces):
            window[micro, number * rows : (number + 1) * rows, :] = piece[
                micro * rows : (micro + 1) * rows, :
            ]


def stacked_heads(ref, micro, rows, kv_head):
    group = HEADS // KV_HEADS
    return jnp.concatenate(
        [
            ref[micro * rows : (micro + 1) * rows, head * HEAD : (head + 1) * HEAD]
            for head in range(kv_head * group, (kv_head + 1) * group)
        ],
        axis=0,
    )


def shares_of(queries, keys, bias):
    scores = lax.dot_general(
        queries, keys, (((1,), (1,)), ((), ())), preferred_element_type=jnp.float32
    ) * HEAD ** (-0.5)
    group = HEADS // KV_HEADS
    rows, span = bias.shape
    scores = scores.reshape(group, rows, span) + bias[None]
    powers = jnp.exp(scores - jnp.max(scores, axis=-1, keepdims=True))
    shares = powers / jnp.sum(powers, axis=-1, keepdims=True)
    return shares.reshape(group * rows, span)


def forward_kernel(
    states,
    query,
    pair_two,
    pair_one,
    pair_own,
    bias,
    gain,
    w_out,
    w_gate,
    w_up,
    w_down,
    output,
    attended,
    mixed,
    normed_two,
    gate,
    up,
    hidden,
    window,
):
    group = HEADS // KV_HEADS
    fill_window(window, (pair_two, pair_one, pair_own))
    micro_count, rows, _ = bias.shape
    for micro in range(micro_count):
        for kv_head in range(KV_HEADS):
            keys = window[micro, :, KEY_AT[kv_head] : KEY_AT[kv_head] + HEAD]
            values = window[micro, :, VALUE_AT[kv_head] : VALUE_AT[kv_head] + HEAD]
            shares = shares_of(stacked_heads(query, micro, rows, kv_head), keys, bias[micro])
            got = jnp.dot(
                shares.astype(jnp.bfloat16), values, preferred_element_type=jnp.float32
            ).astype(jnp.bfloat16)
            for number in range(group):
                head = kv_head * group + number
                attended[micro * rows : (micro + 1) * rows, head * HEAD : (head + 1) * HEAD] = got[
                    number * rows : (number + 1) * rows, :
                ]
    middle = states[...].astype(jnp.float32) + jnp.dot(
        attended[...], w_out[...], preferred_element_type=jnp.float32
    )
    mixed[...] = middle
    low_rows = (middle * rms_scale(middle) * gain[1:2, :]).astype(jnp.bfloat16)
    normed_two[...] = low_rows
    width = FF // 3
    for part in range(3):
        at = slice(part * width, (part + 1) * width)
        gates = jnp.dot(low_rows, w_gate[:, at], preferred_element_type=jnp.float32)
        ups = jnp.dot(low_rows, w_up[:, at], preferred_element_type=jnp.float32)
        gate[:, at] = gates
        up[:, at] = ups
        hidden[:, at] = (gates * jax.nn.sigmoid(gates) * ups).astype(jnp.bfloat16)
    output[...] = (
        mixed[...] + jnp.dot(hidden[...], w_down[...], preferred_element_type=jnp.float32)
    ).astype(jnp.bfloat16)


def against(left, right):
    return lax.dot_general(left, right, (((1,), (1,)), ((), ())), preferred_element_type=jnp.float32)


def across(left, right):
    return lax.dot_general(left, right, (((0,), (0,)), ((), ())), preferred_element_type=jnp.float32)


def backward_kernel(
    grad_output,
    query,
    pair_two,
    pair_one,
    pair_own,
    bias,
    gain,
    mixed,
    gate,
    up,
    w_out,
    w_gate,
    w_up,
    w_down,
    grad_gate,
    grad_up,
    grad_mixed,
    grad_mixed_low,
    grad_query,
    grad_two,
    grad_one,
    grad_own,
    gain_grad,
    window,
    grad_attended,
):
    group = HEADS // KV_HEADS
    fill_window(window, (pair_two, pair_one, pair_own))
    width = FF // 3
    grads = grad_output[...]
    for part in range(3):
        at = slice(part * width, (part + 1) * width)
        grad_hidden = against(grads, w_down[at, :])
        gates = gate[:, at]
        sigmoid = jax.nn.sigmoid(gates)
        grad_gate[:, at] = (
            grad_hidden * up[:, at] * sigmoid * (1.0 + gates * (1.0 - sigmoid))
        ).astype(jnp.bfloat16)
        grad_up[:, at] = (grad_hidden * gates * sigmoid).astype(jnp.bfloat16)
    grad_normed = against(grad_gate[...], w_gate[...]) + against(grad_up[...], w_up[...])
    middle = mixed[...]
    scale = rms_scale(middle)
    gain_grad[...] = jnp.broadcast_to(
        jnp.sum(middle * scale * grad_normed, axis=0, keepdims=True), gain_grad.shape
    )
    grad_middle = grads.astype(jnp.float32) + rms_back(middle, scale, gain[1:2, :], grad_normed)
    grad_mixed[...] = grad_middle
    low_rows = grad_middle.astype(jnp.bfloat16)
    grad_mixed_low[...] = low_rows
    grad_attended[...] = against(low_rows, w_out[...]).astype(jnp.bfloat16)
    micro_count, rows, _ = bias.shape
    for micro in range(micro_count):
        here = slice(micro * rows, (micro + 1) * rows)
        for kv_head in range(KV_HEADS):
            key_at = slice(KEY_AT[kv_head], KEY_AT[kv_head] + HEAD)
            value_at = slice(VALUE_AT[kv_head], VALUE_AT[kv_head] + HEAD)
            keys = window[micro, :, key_at]
            values = window[micro, :, value_at]
            queries = stacked_heads(query, micro, rows, kv_head)
            coming = stacked_heads(grad_attended, micro, rows, kv_head)
            shares = shares_of(queries, keys, bias[micro])
            grad_shares = against(coming, values)
            inner = jnp.sum(shares * grad_shares, axis=-1, keepdims=True)
            grad_scores = (shares * (grad_shares - inner)).astype(jnp.bfloat16)
            got = jnp.dot(grad_scores, keys, preferred_element_type=jnp.float32) * HEAD ** (-0.5)
            for number in range(group):
                head = kv_head * group + number
                grad_query[here, head * HEAD : (head + 1) * HEAD] = got[
                    number * rows : (number + 1) * rows, :
                ]
            grad_keys = across(grad_scores, queries) * HEAD ** (-0.5)
            grad_values = across(shares.astype(jnp.bfloat16), coming)
            for lane_at, item in ((key_at, grad_keys), (value_at, grad_values)):
                grad_two[here, lane_at] = item[:rows].astype(jnp.bfloat16)
                grad_one[here, lane_at] = item[rows : 2 * rows].astype(jnp.bfloat16)
                grad_own[here, lane_at] = item[2 * rows :]


def close_kernel(
    states_ref,
    grad_query,
    grad_own,
    got_one,
    got_two,
    grad_mixed,
    cosine,
    sine,
    gain,
    joined,
    grad_joined,
    grad_states,
    gain_grad,
):
    pair = (
        grad_own[...]
        + got_one[...].astype(jnp.float32)
        + got_two[...].astype(jnp.float32)
    )
    low = lane_low(pair.shape[0])
    tail = swap_halves(lanes(pair, 2))
    blocks = [grad_query[:, number * LANES : (number + 1) * LANES] for number in range(5)]
    blocks[4] = jnp.where(low, blocks[4], tail)
    blocks.append(lanes(pair, 0))
    back = -sine[...]
    blocks = [turned(block, cosine[...], back) for block in blocks]
    blocks.append(lanes(pair, 1))
    blocks.append(jnp.where(low, tail, 0.0))
    for number, block in enumerate(blocks):
        grad_joined[:, number * LANES : (number + 1) * LANES] = block.astype(jnp.bfloat16)
    grad_normed = against(grad_joined[...], joined[...])
    states = states_ref[...].astype(jnp.float32)
    scale = rms_scale(states)
    gain_grad[...] = jnp.broadcast_to(
        jnp.sum(states * scale * grad_normed, axis=0, keepdims=True), gain_grad.shape
    )
    grad_states[...] = (
        grad_mixed[...] + rms_back(states, scale, gain[0:1, :], grad_normed)
    ).astype(jnp.bfloat16)


def on_core(kernel, shapes, scratch, *operands):
    return pl.pallas_call(
        kernel,
        out_shape=tuple(jax.ShapeDtypeStruct(shape, dtype) for shape, dtype in shapes),
        in_specs=in_vmem(len(operands)),
        out_specs=tuple(in_vmem(len(shapes))),
        scratch_shapes=scratch,
        compiler_params=pltpu.CompilerParams(vmem_limit_bytes=VMEM_LIMIT),
    )(*operands)


def layer_forward(states, mats, gain_pair, tables):
    joined, w_out, w_gate, w_up, w_down = mats
    cosine, sine, bias = tables
    rows = states.shape[0]
    low, wide = jnp.bfloat16, jnp.float32
    normed, query, pair = on_core(
        project_kernel,
        [((rows, D), low), ((rows, KEY_MAIN), low), ((rows, 3 * LANES), low)],
        [],
        states,
        gain_pair,
        joined,
        cosine,
        sine,
    )
    window = (passed_along(pair, "fsdp", 2), passed_along(pair, "fsdp", 1), pair)
    output, attended, mixed, normed_two, gate, up, hidden = on_core(
        forward_kernel,
        [
            ((rows, D), low),
            ((rows, D), low),
            ((rows, D), wide),
            ((rows, D), low),
            ((rows, FF), wide),
            ((rows, FF), wide),
            ((rows, FF), low),
        ],
        [pltpu.VMEM((bias.shape[0], bias.shape[2], 3 * LANES), low)],
        states,
        query,
        *window,
        bias,
        gain_pair,
        w_out,
        w_gate,
        w_up,
        w_down,
    )
    return output, (normed, query, window, attended, mixed, normed_two, gate, up, hidden)


def layer_backward(grad_output, states, kept, mats, gain_pair, tables):
    joined, w_out, w_gate, w_up, w_down = mats
    cosine, sine, bias = tables
    normed, query, window, attended, mixed, normed_two, gate, up, hidden = kept
    rows = states.shape[0]
    low, wide = jnp.bfloat16, jnp.float32
    pair_shape = (rows, 3 * LANES)
    (
        grad_gate,
        grad_up,
        grad_mixed,
        grad_mixed_low,
        grad_query,
        grad_two,
        grad_one,
        grad_own,
        gain_two,
    ) = on_core(
        backward_kernel,
        [
            ((rows, FF), low),
            ((rows, FF), low),
            ((rows, D), wide),
            ((rows, D), low),
            ((rows, KEY_MAIN), wide),
            (pair_shape, low),
            (pair_shape, low),
            (pair_shape, wide),
            ((8, D), wide),
        ],
        [
            pltpu.VMEM((bias.shape[0], bias.shape[2], 3 * LANES), low),
            pltpu.VMEM((rows, D), low),
        ],
        grad_output,
        query,
        *window,
        bias,
        gain_pair,
        mixed,
        gate,
        up,
        w_out,
        w_gate,
        w_up,
        w_down,
    )
    grad_joined, grad_states, gain_one = on_core(
        close_kernel,
        [((rows, SLOTS), low), ((rows, D), low), ((8, D), wide)],
        [],
        states,
        grad_query,
        grad_own,
        passed_along(grad_one, "fsdp", -1),
        passed_along(grad_two, "fsdp", -2),
        grad_mixed,
        cosine,
        sine,
        gain_pair,
        joined,
    )
    factors = (
        normed,
        attended,
        normed_two,
        hidden,
        grad_joined,
        grad_mixed_low,
        grad_gate,
        grad_up,
        grad_output,
    )
    return grad_states, factors, jnp.concatenate([gain_one[0], gain_two[0]])


def local(ends, weights, gains, segments):
    micro_count = ends.shape[1]
    rows = ends.shape[2]
    first = lax.axis_index("section") == 0
    mats, gain_pair = gather_layer(weights, gains)
    marked = segments + 1
    rims = [passed_along(marked, "fsdp", 2), passed_along(marked, "fsdp", 1), marked]
    window_segments = jnp.concatenate(rims, axis=1)
    span = window_segments.shape[1]
    place = jnp.arange(span, dtype=jnp.int32)
    change = jnp.concatenate(
        [jnp.ones((micro_count, 1), dtype=bool), window_segments[:, 1:] != window_segments[:, :-1]],
        axis=1,
    )
    starts = lax.cummax(jnp.where(change, place[None, :], 0), axis=1)
    positions = (place[None, :] - starts)[:, span - rows :].reshape(-1)
    cosine, sine = rope_tables(positions)
    cosine = jnp.concatenate([cosine] * 4, axis=1)
    sine = jnp.concatenate([-sine, sine, -sine, sine], axis=1)
    allowed = (window_segments[:, span - rows :, None] == window_segments[:, None, :]) & (
        place[None, None, :] <= place[None, span - rows :, None]
    )
    bias = jnp.where(allowed, 0.0, masked_score).astype(jnp.float32)
    tables = (cosine, sine, bias)
    own = ends[0].reshape(micro_count * rows, D)
    middle, _ = layer_forward(own, mats, gain_pair, tables)
    states = jnp.where(first, own, passed_along(middle, "section", 1))
    output, kept = layer_forward(states, mats, gain_pair, tables)
    grad_middle, _, _ = layer_backward(own, states, kept, mats, gain_pair, tables)
    grad_output = jnp.where(first, passed_along(grad_middle, "section", -1), own)
    grad_states, factors, gain_grad = layer_backward(
        grad_output, states, kept, mats, gain_pair, tables
    )
    weight_share, gain_share = reduce_terms(factors, gain_grad)
    ends_out = jnp.where(first, grad_states, output).reshape(ends.shape)
    return (ends_out, weight_share[None], gain_share[None])


def solution(mesh):
    placed = (
        P("section", None, "fsdp", None),
        P("section", "fsdp"),
        P("section", "fsdp"),
        P(None, "fsdp"),
    )
    return jax.shard_map(
        local,
        mesh=mesh,
        in_specs=placed,
        out_specs=(P("section", None, "fsdp", None), P("section", "fsdp"), P("section", "fsdp")),
        check_vma=False,
    )
```

```python
import jax
import jax.numpy as jnp
from jax import lax
from jax.experimental import pallas as pl
from jax.experimental.pallas import tpu as pltpu
from jax.sharding import PartitionSpec as P

D = 576
HEADS = 9
KV_HEADS = 3
HEAD = 64
FF = 1536
REACH = 2


epsilon = 1e-05
rope_base = 100000.0
masked_score = -1e30


def passed_along(value, axis, steps):
    count = lax.axis_size(axis)
    first, last = (max(0, -steps), min(count, count - steps))
    return lax.ppermute(value, axis, [(source, source + steps) for source in range(first, last)])


def rope_tables(positions):
    half = HEAD // 2
    frequency = rope_base ** (-2.0 * jnp.arange(half, dtype=jnp.float32) / HEAD)
    angles = positions.astype(jnp.float32)[:, None] * frequency[None, :]
    return (jnp.cos(angles), jnp.sin(angles))


def rms_scale(states):
    return lax.rsqrt(jnp.mean(states * states, axis=-1, keepdims=True) + epsilon)


def rms_back(states, scale, gain, grad):
    weighted = grad * gain
    return scale * weighted - states * (scale * scale * scale) * jnp.mean(
        weighted * states, axis=-1, keepdims=True
    )


def unpack(flat_vector):
    query_cols = HEADS * HEAD
    kv_cols = KV_HEADS * HEAD
    shapes = [
        (D, query_cols),
        (D, kv_cols),
        (D, kv_cols),
        (query_cols, D),
        (D, FF),
        (D, FF),
        (FF, D),
    ]
    pieces = []
    offset = 0
    for row_count, col_count in shapes:
        pieces.append(
            flat_vector[offset : offset + row_count * col_count].reshape(row_count, col_count)
        )
        offset = offset + row_count * col_count
    return pieces


LANES = 128
SHARD_ROWS = 1728
GAIN_ROWS = 16
BLOCK_ROWS = SHARD_ROWS + GAIN_ROWS
PIECE_ROWS = 864
VMEM_LIMIT = 20 * 1024 * 1024


def lane_low(rows):
    return lax.broadcasted_iota(jnp.int32, (rows, LANES), 1) < 64


def swap_halves(value):
    return pltpu.roll(value, 64, 1)


def narrow_pack(wide, natural, out_ref, start, columns):
    full = columns // LANES
    period = 2 * full + 1
    pairs = PIECE_ROWS // period
    low = lane_low(pairs)
    part = [wide[pl.ds(start + j, pairs, stride=period), :] for j in range(period)]
    at = start
    for c in range(full):
        natural[pl.ds(0, pairs, stride=2), :] = part[c]
        natural[pl.ds(1, pairs, stride=2), :] = swap_halves(
            jnp.where(low, part[full + c + 1], part[full + c])
        )
        out_ref[at : at + 2 * pairs, :] = natural[0 : 2 * pairs, :].astype(jnp.bfloat16)
        at += 2 * pairs
    natural[pl.ds(0, pairs, stride=2), :] = part[full]
    natural[pl.ds(1, pairs, stride=2), :] = swap_halves(part[2 * full])
    out_ref[at : at + pairs, :] = jnp.where(
        low, natural[0:pairs, :], swap_halves(natural[pairs : 2 * pairs, :])
    ).astype(jnp.bfloat16)


def narrow_unpack(packed, natural, out_ref, start, columns):
    full = columns // LANES
    period = 2 * full + 1
    pairs = PIECE_ROWS // period
    low = lane_low(pairs)
    evens, odds = [], []
    at = start
    for c in range(full):
        natural[0 : 2 * pairs, :] = packed[at : at + 2 * pairs, :]
        evens.append(natural[pl.ds(0, pairs, stride=2), :])
        odds.append(swap_halves(natural[pl.ds(1, pairs, stride=2), :]))
        at += 2 * pairs
    tail = packed[at : at + pairs, :]
    natural[0:pairs, :] = tail
    natural[pairs : 2 * pairs, :] = swap_halves(tail)
    tail_even = natural[pl.ds(0, pairs, stride=2), :]
    tail_odd = swap_halves(natural[pl.ds(1, pairs, stride=2), :])
    rows = evens + [jnp.where(low, tail_even, odds[0])]
    for c in range(full - 1):
        rows.append(jnp.where(low, odds[c], odds[c + 1]))
    rows.append(jnp.where(low, odds[full - 1], tail_odd))
    for j in range(period):
        out_ref[pl.ds(start + j, pairs, stride=period), :] = rows[j]


def by_owner(owner, narrow, wide):
    @pl.when((owner == 0) | (owner == 3) | (owner >= 12))
    def _():
        narrow(0, D)
        narrow(PIECE_ROWS, D)

    @pl.when(owner == 1)
    def _():
        narrow(0, D)
        narrow(PIECE_ROWS, KV_HEADS * HEAD)

    @pl.when(owner == 2)
    def _():
        narrow(0, KV_HEADS * HEAD)
        narrow(PIECE_ROWS, D)

    @pl.when((owner >= 4) & (owner < 12))
    def _():
        wide()


def pack_kernel(owner_ref, flat_ref, gain_ref, *refs):
    count = len(GATHER_CUTS) - 1
    chunks = refs[:count]
    wide, natural, block = refs[count:]
    for number in range(SHARD_ROWS):
        wide[number : number + 1, :] = flat_ref[
            0:1, number * LANES : (number + 1) * LANES
        ].astype(jnp.float32)
    block[SHARD_ROWS:BLOCK_ROWS, :] = gain_ref[...]

    def narrow(start, columns):
        narrow_pack(wide, natural, block, start, columns)

    def broad():
        blocks = FF // LANES
        rows = SHARD_ROWS // blocks
        for c in range(blocks):
            block[c * rows : (c + 1) * rows, :] = wide[pl.ds(c, rows, stride=blocks), :].astype(
                jnp.bfloat16
            )

    by_owner(owner_ref[0], narrow, broad)
    for number in range(count):
        chunks[number][...] = block[GATHER_CUTS[number] : GATHER_CUTS[number + 1], :]


def pack_shard(owner, flat, gain_rows):
    sizes = [GATHER_CUTS[n + 1] - GATHER_CUTS[n] for n in range(len(GATHER_CUTS) - 1)]
    return pl.pallas_call(
        pack_kernel,
        out_shape=tuple(jax.ShapeDtypeStruct((size, LANES), jnp.bfloat16) for size in sizes),
        in_specs=[pl.BlockSpec(memory_space=pltpu.SMEM)] + in_vmem(2),
        out_specs=tuple(in_vmem(len(sizes))),
        scratch_shapes=[
            pltpu.VMEM((SHARD_ROWS, LANES), jnp.float32),
            pltpu.VMEM((1152, LANES), jnp.float32),
            pltpu.VMEM((BLOCK_ROWS, LANES), jnp.bfloat16),
        ],
        compiler_params=pltpu.CompilerParams(vmem_limit_bytes=VMEM_LIMIT),
        cost_estimate=pl.CostEstimate(flops=6_000_000_000, bytes_accessed=0, transcendentals=0),
    )(owner, flat, gain_rows)


def finish_kernel(owner_ref, *refs):
    count = len(REDUCE_CUTS) - 1
    kept_refs, got_refs = refs[:count], refs[count : 2 * count]
    out_ref, gain_ref, total, natural = refs[2 * count :]
    for number in range(count):
        total[REDUCE_CUTS[number] : REDUCE_CUTS[number + 1], :] = kept_refs[number][
            ...
        ].astype(jnp.float32) + got_refs[number][...].astype(jnp.float32)
    gain_ref[...] = total[SHARD_ROWS:, :]

    def narrow(start, columns):
        narrow_unpack(total, natural, out_ref, start, columns)

    def broad():
        blocks = FF // LANES
        rows = SHARD_ROWS // blocks
        for c in range(blocks):
            out_ref[pl.ds(c, rows, stride=blocks), :] = total[c * rows : (c + 1) * rows, :]

    by_owner(owner_ref[0], narrow, broad)


def in_vmem(count):
    return [pl.BlockSpec(memory_space=pltpu.VMEM)] * count


def finish_shard(owner, kept, got):
    return pl.pallas_call(
        finish_kernel,
        out_shape=(
            jax.ShapeDtypeStruct((SHARD_ROWS, LANES), jnp.float32),
            jax.ShapeDtypeStruct((GAIN_ROWS, LANES), jnp.float32),
        ),
        in_specs=[pl.BlockSpec(memory_space=pltpu.SMEM)] + in_vmem(len(kept) + len(got)),
        out_specs=tuple(in_vmem(2)),
        scratch_shapes=[
            pltpu.VMEM((BLOCK_ROWS, LANES), jnp.float32),
            pltpu.VMEM((1152, LANES), jnp.float32),
        ],
        compiler_params=pltpu.CompilerParams(vmem_limit_bytes=VMEM_LIMIT),
        cost_estimate=pl.CostEstimate(flops=6_000_000_000, bytes_accessed=0, transcendentals=0),
    )(owner, *kept, *got)


SLOTS = 1024
KEY_MAIN = 640
KEY_TAIL = 576
VALUE_MAIN = 768
VALUE_TAIL = 896
GATHER_CUTS = (0, 544, 1088, 1408, 1744)
GATHER_ORDERS = ((8, 4, 2, 1), (4, 8, 1, 2), (2, 1, 8, 4), (1, 2, 4, 8))
REDUCE_CUTS = (0, 320, 640, 1088, 1408, 1744)
REDUCE_ORDERS = (
    (1, 2, 4, 8),
    (2, 1, 4, 8),
    (4, 8, 1, 2),
    (1, 2, 4, 8),
    (2, 1, 4, 8),
)


def place_narrow(block, at, target, row, main, tail, columns):
    full = columns // LANES
    pairs = PIECE_ROWS // (2 * full + 1)
    for c in range(full):
        target[pl.ds(row, 2 * pairs), main + c * LANES : main + (c + 1) * LANES] = block[
            at : at + 2 * pairs, :
        ]
        at += 2 * pairs
    target[pl.ds(row, pairs), tail : tail + 64] = block[at : at + pairs, :64]
    target[pl.ds(row + pairs, pairs), tail : tail + 64] = block[at : at + pairs, 64:]


def place_kernel(index_ref, *refs):
    count = len(GATHER_CUTS) - 1
    chunks = refs[:count]
    joined, out, gate, up, down, gain, block = refs[count:]
    owner = pl.program_id(0)
    kv_width = KV_HEADS * HEAD
    for number in range(count):
        block[GATHER_CUTS[number] : GATHER_CUTS[number + 1], :] = chunks[number][
            index_ref[number, owner]
        ]
    gain[pl.ds(pl.multiple_of(owner * GAIN_ROWS, GAIN_ROWS), GAIN_ROWS), :] = block[SHARD_ROWS:, :]

    @pl.when(owner == 0)
    def _():
        joined[:, SLOTS - 128 :] = jnp.zeros((D, 128), jnp.bfloat16)
        place_narrow(block, 0, joined, 0, 0, 512, D)
        place_narrow(block, PIECE_ROWS, joined, 192, 0, 512, D)

    @pl.when(owner == 1)
    def _():
        place_narrow(block, 0, joined, 384, 0, 512, D)
        place_narrow(block, PIECE_ROWS, joined, 0, KEY_MAIN, KEY_TAIL, kv_width)

    @pl.when(owner == 2)
    def _():
        place_narrow(block, 0, joined, 0, VALUE_MAIN, VALUE_TAIL, kv_width)
        place_narrow(block, PIECE_ROWS, out, 0, 0, 512, D)

    @pl.when(owner == 3)
    def _():
        place_narrow(block, 0, out, 192, 0, 512, D)
        place_narrow(block, PIECE_ROWS, out, 384, 0, 512, D)

    def broad(target, first):
        @pl.when((owner >= first) & (owner < first + 4))
        def _():
            row = pl.multiple_of((owner - first) * 144, 16)
            for c in range(FF // LANES):
                target[pl.ds(row, 144), c * LANES : (c + 1) * LANES] = block[
                    c * 144 : (c + 1) * 144, :
                ]

    broad(gate, 4)
    broad(up, 8)

    @pl.when(owner >= 12)
    def _():
        row = pl.multiple_of((owner - 12) * 384, 16)
        place_narrow(block, 0, down, row, 0, 512, D)
        place_narrow(block, PIECE_ROWS, down, pl.multiple_of(row + 192, 16), 0, 512, D)


def place_blocks(index, chunks):
    shapes = [(D, SLOTS), (D, D), (D, FF), (D, FF), (FF, D), (16 * GAIN_ROWS, LANES)]
    return pl.pallas_call(
        place_kernel,
        out_shape=tuple(jax.ShapeDtypeStruct(shape, jnp.bfloat16) for shape in shapes),
        grid=(16,),
        in_specs=[pl.BlockSpec(memory_space=pltpu.SMEM)] + in_vmem(len(chunks)),
        out_specs=tuple(in_vmem(len(shapes))),
        scratch_shapes=[pltpu.VMEM((BLOCK_ROWS, LANES), jnp.bfloat16)],
        compiler_params=pltpu.CompilerParams(vmem_limit_bytes=VMEM_LIMIT),
        cost_estimate=pl.CostEstimate(flops=6_000_000_000, bytes_accessed=0, transcendentals=0),
    )(index, *chunks)


def store_narrow(result, block, at, main, tail, columns):
    full = columns // LANES
    pairs = PIECE_ROWS // (2 * full + 1)
    for c in range(full):
        block[at : at + 2 * pairs, :] = result[
            :, main + c * LANES : main + (c + 1) * LANES
        ].astype(jnp.bfloat16)
        at += 2 * pairs
    block[at : at + pairs, :] = jnp.concatenate(
        [result[:pairs, tail : tail + 64], result[pairs:, tail : tail + 64]], axis=1
    ).astype(jnp.bfloat16)


def send_blocks(index_ref, outs, block, sems, owner, plain):
    waits = []
    for number in range(len(REDUCE_CUTS) - 1):
        first, last = REDUCE_CUTS[number], REDUCE_CUTS[number + 1]
        rows = min(last, SHARD_ROWS) - first if plain else last - first
        place = index_ref[number, owner]
        for half in range(2):
            copy = pltpu.make_async_copy(
                block.at[first : first + rows, :],
                outs[2 * number + half].at[lax.rem(place, 8), 0:rows, :],
                sems.at[number],
            )
            chosen = place >= 8 if half else place < 8
            pl.when(chosen)(copy.start)
            waits.append((chosen, copy.wait))
    return waits


def turned_product(turned_ref, row, count, right):
    return jnp.dot(turned_ref[row : row + count, :], right, preferred_element_type=jnp.float32)


def wide_terms_kernel(
    index_ref, attended, normed_two, hidden, grad_mixed, grad_gate, grad_up, grad_output, *refs
):
    outs = refs[: 2 * (len(REDUCE_CUTS) - 1)]
    blocks, attended_t, normed_two_t, hidden_t, sems = refs[len(outs) :]
    waits = []
    normed_two_t[...] = normed_two[...].T
    for number, right in ((0, grad_gate), (1, grad_up)):
        for part in range(4):
            owner = 4 + 4 * number + part
            block = blocks.at[owner - 3]
            result = turned_product(normed_two_t, 144 * part, 144, right[...]).astype(jnp.bfloat16)
            for c in range(FF // LANES):
                block[c * 144 : (c + 1) * 144, :] = result[:, c * LANES : (c + 1) * LANES]
            waits += send_blocks(index_ref, outs, block, sems.at[owner - 3], owner, True)
    hidden_t[...] = hidden[...].T
    for part in range(4):
        owner = 12 + part
        block = blocks.at[owner - 3]
        for half in range(2):
            result = turned_product(hidden_t, 384 * part + 192 * half, 192, grad_output[...])
            store_narrow(result, block, half * PIECE_ROWS, 0, 512, D)
        waits += send_blocks(index_ref, outs, block, sems.at[owner - 3], owner, True)
    attended_t[...] = attended[...].T
    block = blocks.at[0]
    for half in range(2):
        result = turned_product(attended_t, 192 + 192 * half, 192, grad_mixed[...])
        store_narrow(result, block, half * PIECE_ROWS, 0, 512, D)
    waits += send_blocks(index_ref, outs, block, sems.at[0], 3, True)
    for chosen, wait in waits:
        pl.when(chosen)(wait)


def narrow_terms_kernel(index_ref, normed, attended, grad_joined, grad_mixed, gain_ref, *refs):
    count = len(REDUCE_CUTS) - 1
    outs = refs[2 * count : 4 * count]
    blocks, normed_t, attended_t, sems, gain_sems = refs[4 * count :]
    kv_width = KV_HEADS * HEAD
    waits = []
    place_rows = REDUCE_CUTS[-1] - REDUCE_CUTS[-2]
    for owner in range(3, 16):
        place = index_ref[count - 1, owner]
        for half in range(2):
            copy = pltpu.make_async_copy(
                gain_ref.at[owner],
                outs[2 * count - 2 + half].at[
                    lax.rem(place, 8), place_rows - GAIN_ROWS : place_rows, :
                ],
                gain_sems.at[owner],
            )
            chosen = place >= 8 if half else place < 8
            pl.when(chosen)(copy.start)
            waits.append((chosen, copy.wait))
    normed_t[...] = normed[...].T
    attended_t[...] = attended[...].T
    query = grad_joined[:, :KEY_MAIN]
    for owner in range(3):
        block = blocks.at[owner]
        block[SHARD_ROWS:BLOCK_ROWS, :] = gain_ref[owner]
        if owner == 0:
            for half in range(2):
                result = turned_product(normed_t, 192 * half, 192, query)
                store_narrow(result, block, half * PIECE_ROWS, 0, 512, D)
        elif owner == 1:
            store_narrow(turned_product(normed_t, 384, 192, query), block, 0, 0, 512, D)
            key = turned_product(normed_t, 0, D, grad_joined[:, 512:768])
            store_narrow(key, block, PIECE_ROWS, KEY_MAIN - 512, KEY_TAIL - 512, kv_width)
        else:
            value = turned_product(normed_t, 0, D, grad_joined[:, VALUE_MAIN:])
            store_narrow(value, block, 0, 0, VALUE_TAIL - VALUE_MAIN, kv_width)
            result = turned_product(attended_t, 0, 192, grad_mixed[...])
            store_narrow(result, block, PIECE_ROWS, 0, 512, D)
        waits += send_blocks(index_ref, outs, block, sems.at[owner], owner, False)
    for chosen, wait in waits:
        pl.when(chosen)(wait)


def half_shapes():
    return tuple(
        jax.ShapeDtypeStruct((8, REDUCE_CUTS[n + 1] - REDUCE_CUTS[n], LANES), jnp.bfloat16)
        for n in range(len(REDUCE_CUTS) - 1)
        for _ in range(2)
    )


def wide_terms(index, factors):
    shapes = half_shapes()
    rows = factors[0].shape[0]
    return pl.pallas_call(
        wide_terms_kernel,
        out_shape=shapes,
        in_specs=[pl.BlockSpec(memory_space=pltpu.SMEM)] + in_vmem(len(factors)),
        out_specs=tuple(pl.BlockSpec(memory_space=pl.ANY) for _ in shapes),
        scratch_shapes=[
            pltpu.VMEM((13, BLOCK_ROWS, LANES), jnp.bfloat16),
            pltpu.VMEM((D, rows), jnp.bfloat16),
            pltpu.VMEM((D, rows), jnp.bfloat16),
            pltpu.VMEM((FF, rows), jnp.bfloat16),
            pltpu.SemaphoreType.DMA((13, len(REDUCE_CUTS) - 1)),
        ],
        compiler_params=pltpu.CompilerParams(vmem_limit_bytes=VMEM_LIMIT),
        cost_estimate=pl.CostEstimate(flops=6_000_000_000, bytes_accessed=0, transcendentals=0),
    )(index, *factors)


def narrow_terms(index, factors, gain_rows, halves):
    shapes = half_shapes()
    rows = factors[0].shape[0]
    lead = 2 + len(factors)
    return pl.pallas_call(
        narrow_terms_kernel,
        out_shape=shapes,
        in_specs=[pl.BlockSpec(memory_space=pltpu.SMEM)]
        + in_vmem(len(factors) + 1)
        + [pl.BlockSpec(memory_space=pl.ANY) for _ in shapes],
        out_specs=tuple(pl.BlockSpec(memory_space=pl.ANY) for _ in shapes),
        input_output_aliases={lead + n: n for n in range(len(shapes))},
        scratch_shapes=[
            pltpu.VMEM((3, BLOCK_ROWS, LANES), jnp.bfloat16),
            pltpu.VMEM((D, rows), jnp.bfloat16),
            pltpu.VMEM((D, rows), jnp.bfloat16),
            pltpu.SemaphoreType.DMA((3, len(REDUCE_CUTS) - 1)),
            pltpu.SemaphoreType.DMA((16,)),
        ],
        compiler_params=pltpu.CompilerParams(vmem_limit_bytes=VMEM_LIMIT),
        cost_estimate=pl.CostEstimate(flops=6_000_000_000, bytes_accessed=0, transcendentals=0),
    )(index, *factors, gain_rows, *halves)


def partner(value, stride):
    count = lax.axis_size("fsdp")
    return lax.ppermute(value, "fsdp", [(source, source ^ stride) for source in range(count)])


def block_index(orders, first_is_low):
    apart = jnp.arange(16, dtype=jnp.int32) ^ lax.axis_index("fsdp").astype(jnp.int32)
    rows = []
    for order in orders:
        place = jnp.zeros_like(apart)
        for stage, stride in enumerate(order):
            bit = stage if first_is_low else len(order) - 1 - stage
            place = place + jnp.where((apart & stride) != 0, 1 << bit, 0)
        rows.append(place)
    return jnp.stack(rows)


def gather_layer(weights, gains, segments):
    owners = lax.axis_size("fsdp")
    if owners != 16:
        flat_full = lax.all_gather(weights[0], "fsdp", axis=0, tiled=True)
        gain_full = lax.all_gather(gains[0], "fsdp", axis=0, tiled=True)
        query, key, value, out, gate, up, down = unpack(flat_full)
        joined = jnp.concatenate(
            [
                query,
                key[:, LANES:],
                key[:, :LANES],
                value,
                jnp.zeros((D, SLOTS - VALUE_TAIL - 64), jnp.bfloat16),
            ],
            axis=1,
        )
        return (joined, out, gate, up, down), gain_full.astype(jnp.float32).reshape(2, D), segments
    owner = lax.axis_index("fsdp").astype(jnp.int32).reshape(1)
    share = gains.shape[1]
    gain_rows = jnp.pad(gains, ((0, GAIN_ROWS - 1), (0, LANES - share)))
    chunks = list(pack_shard(owner, weights, gain_rows))
    segments, *chunks = lax.optimization_barrier((segments, *chunks))
    for stage in range(4):
        got = [partner(chunk, order[stage]) for chunk, order in zip(chunks, GATHER_ORDERS)]
        chunks = [jnp.concatenate(both) for both in zip(chunks, got)]
    chunks = [chunk.reshape(16, -1, LANES) for chunk in chunks]
    *mats, gain_full = place_blocks(block_index(GATHER_ORDERS, True), chunks)
    gain_full = gain_full.reshape(16, GAIN_ROWS, LANES)[:, 0, :share]
    return tuple(mats), gain_full.astype(jnp.float32).reshape(2, D), segments


def reduce_terms(factors, gain_grad, halves):
    owners = lax.axis_size("fsdp")
    share = gain_grad.shape[0] // owners
    if owners != 16:
        normed, attended, normed_two, hidden, joined, grad_mixed, grad_gate, grad_up, last = factors
        pairs = [
            (normed, joined[:, :D]),
            (normed, jnp.concatenate([joined[:, KEY_MAIN:VALUE_MAIN], joined[:, D:KEY_MAIN]], 1)),
            (normed, joined[:, VALUE_MAIN : VALUE_TAIL + 64]),
            (attended, grad_mixed),
            (normed_two, grad_gate),
            (normed_two, grad_up),
            (hidden, last),
        ]
        flat_grads = jnp.concatenate(
            [
                jnp.einsum("rd,re->de", left, right, preferred_element_type=jnp.float32).reshape(-1)
                for left, right in pairs
            ]
        )
        got = [
            lax.all_to_all(
                item.reshape(owners, -1).astype(jnp.bfloat16),
                "fsdp",
                split_axis=0,
                concat_axis=0,
                tiled=True,
            ).astype(jnp.float32)
            for item in (flat_grads, gain_grad)
        ]
        return tuple(jnp.sum(item, axis=0) for item in got)
    gain_rows = jnp.pad(
        gain_grad.reshape(owners, 1, share).astype(jnp.bfloat16),
        ((0, 0), (0, GAIN_ROWS - 1), (0, LANES - share)),
    )
    normed, attended, _, _, grad_joined, grad_mixed = factors[:6]
    halves = narrow_terms(
        block_index(REDUCE_ORDERS, False),
        (normed, attended, grad_joined, grad_mixed),
        gain_rows,
        halves,
    )
    kept, sent = halves[0::2], halves[1::2]
    for stage in range(4):
        if stage:
            half = 8 >> stage
            kept, sent = [item[:half] for item in sums], [item[half:] for item in sums]
        got = [partner(item, order[stage]) for item, order in zip(sent, REDUCE_ORDERS)]
        if stage < 3:
            sums = [
                (one.astype(jnp.float32) + other.astype(jnp.float32)).astype(jnp.bfloat16)
                for one, other in zip(kept, got)
            ]
    owner = lax.axis_index("fsdp").astype(jnp.int32).reshape(1)
    flat, gain = finish_shard(owner, [item[0] for item in kept], [item[0] for item in got])
    return flat.reshape(-1), gain[0, :share]


def turned(block, cosine, sine):
    low = lax.broadcasted_iota(jnp.int32, block.shape, 1) % 64 < 32
    other = jnp.where(low, pltpu.roll(block, 96, 1), pltpu.roll(block, 32, 1))
    return block * cosine + other * sine


def lanes(value, number):
    return value[:, number * LANES : (number + 1) * LANES]


def project_kernel(states_ref, gain, joined, cosine, sine, normed, query, pair):
    states = states_ref[...].astype(jnp.float32)
    low_rows = (states * rms_scale(states) * gain[0:1, :]).astype(jnp.bfloat16)
    normed[...] = low_rows
    full = jnp.dot(low_rows, joined[...], preferred_element_type=jnp.float32)
    blocks = [turned(lanes(full, number), cosine[...], sine[...]) for number in range(6)]
    for number in range(5):
        query[:, number * LANES : (number + 1) * LANES] = blocks[number].astype(jnp.bfloat16)
    low = lane_low(full.shape[0])
    pair[:, :LANES] = blocks[5].astype(jnp.bfloat16)
    pair[:, LANES : 2 * LANES] = lanes(full, 6).astype(jnp.bfloat16)
    pair[:, 2 * LANES :] = jnp.where(
        low, swap_halves(blocks[4]), swap_halves(lanes(full, 7))
    ).astype(jnp.bfloat16)


KEY_AT = (0, 64, 256)
VALUE_AT = (128, 192, 320)


def fill_window(window, pieces):
    micro_count, span, _ = window.shape
    rows = span // len(pieces)
    for micro in range(micro_count):
        for number, piece in enumerate(pieces):
            window[micro, number * rows : (number + 1) * rows, :] = piece[
                micro * rows : (micro + 1) * rows, :
            ]


def stacked_heads(ref, micro, rows, kv_head):
    group = HEADS // KV_HEADS
    return jnp.concatenate(
        [
            ref[micro * rows : (micro + 1) * rows, head * HEAD : (head + 1) * HEAD]
            for head in range(kv_head * group, (kv_head + 1) * group)
        ],
        axis=0,
    )


def shares_of(queries, keys, bias):
    scores = lax.dot_general(
        queries, keys, (((1,), (1,)), ((), ())), preferred_element_type=jnp.float32
    ) * HEAD ** (-0.5)
    group = HEADS // KV_HEADS
    rows, span = bias.shape
    scores = scores.reshape(group, rows, span) + bias[None]
    powers = jnp.exp(scores - jnp.max(scores, axis=-1, keepdims=True))
    shares = powers / jnp.sum(powers, axis=-1, keepdims=True)
    return shares.reshape(group * rows, span)


def forward_kernel(
    states,
    query,
    pair_two,
    pair_one,
    pair_own,
    bias,
    gain,
    w_out,
    w_gate,
    w_up,
    w_down,
    output,
    *refs,
):
    if len(refs) == 7:
        attended, mixed, normed_two, gate, up, hidden, window = refs
    else:
        attended, mixed, hidden, window = refs
        normed_two = gate = up = None
    group = HEADS // KV_HEADS
    fill_window(window, (pair_two, pair_one, pair_own))
    micro_count, rows, _ = bias.shape
    for micro in range(micro_count):
        for kv_head in range(KV_HEADS):
            keys = window[micro, :, KEY_AT[kv_head] : KEY_AT[kv_head] + HEAD]
            values = window[micro, :, VALUE_AT[kv_head] : VALUE_AT[kv_head] + HEAD]
            shares = shares_of(stacked_heads(query, micro, rows, kv_head), keys, bias[micro])
            got = jnp.dot(
                shares.astype(jnp.bfloat16), values, preferred_element_type=jnp.float32
            ).astype(jnp.bfloat16)
            for number in range(group):
                head = kv_head * group + number
                attended[micro * rows : (micro + 1) * rows, head * HEAD : (head + 1) * HEAD] = got[
                    number * rows : (number + 1) * rows, :
                ]
    middle = states[...].astype(jnp.float32) + jnp.dot(
        attended[...], w_out[...], preferred_element_type=jnp.float32
    )
    mixed[...] = middle
    low_rows = (middle * rms_scale(middle) * gain[1:2, :]).astype(jnp.bfloat16)
    if normed_two is not None:
        normed_two[...] = low_rows
    width = FF // 3
    for part in range(3):
        at = slice(part * width, (part + 1) * width)
        gates = jnp.dot(low_rows, w_gate[:, at], preferred_element_type=jnp.float32)
        ups = jnp.dot(low_rows, w_up[:, at], preferred_element_type=jnp.float32)
        if gate is not None:
            gate[:, at] = gates
            up[:, at] = ups
        hidden[:, at] = (gates * jax.nn.sigmoid(gates) * ups).astype(jnp.bfloat16)
    output[...] = (
        mixed[...] + jnp.dot(hidden[...], w_down[...], preferred_element_type=jnp.float32)
    ).astype(jnp.bfloat16)


def against(left, right):
    return lax.dot_general(left, right, (((1,), (1,)), ((), ())), preferred_element_type=jnp.float32)


def across(left, right):
    return lax.dot_general(left, right, (((0,), (0,)), ((), ())), preferred_element_type=jnp.float32)


def backward_kernel(
    grad_output,
    query,
    pair_two,
    pair_one,
    pair_own,
    bias,
    gain,
    mixed,
    gate,
    up,
    w_out,
    w_gate,
    w_up,
    w_down,
    grad_mixed,
    grad_query,
    grad_two,
    grad_one,
    grad_own,
    *refs,
):
    if len(refs) == 6:
        grad_gate, grad_up, grad_mixed_low, gain_grad, window, grad_attended = refs
    else:
        grad_gate, grad_up, window, grad_attended = refs
        grad_mixed_low = gain_grad = None
    group = HEADS // KV_HEADS
    fill_window(window, (pair_two, pair_one, pair_own))
    width = FF // 3
    grads = grad_output[...]
    for part in range(3):
        at = slice(part * width, (part + 1) * width)
        grad_hidden = against(grads, w_down[at, :])
        gates = gate[:, at]
        sigmoid = jax.nn.sigmoid(gates)
        grad_gate[:, at] = (
            grad_hidden * up[:, at] * sigmoid * (1.0 + gates * (1.0 - sigmoid))
        ).astype(jnp.bfloat16)
        grad_up[:, at] = (grad_hidden * gates * sigmoid).astype(jnp.bfloat16)
    grad_normed = against(grad_gate[...], w_gate[...]) + against(grad_up[...], w_up[...])
    middle = mixed[...]
    scale = rms_scale(middle)
    if gain_grad is not None:
        gain_grad[...] = jnp.broadcast_to(
            jnp.sum(middle * scale * grad_normed, axis=0, keepdims=True), gain_grad.shape
        )
    grad_middle = grads.astype(jnp.float32) + rms_back(middle, scale, gain[1:2, :], grad_normed)
    grad_mixed[...] = grad_middle
    low_rows = grad_middle.astype(jnp.bfloat16)
    if grad_mixed_low is not None:
        grad_mixed_low[...] = low_rows
    grad_attended[...] = against(low_rows, w_out[...]).astype(jnp.bfloat16)
    micro_count, rows, _ = bias.shape
    for micro in range(micro_count):
        here = slice(micro * rows, (micro + 1) * rows)
        for kv_head in range(KV_HEADS):
            key_at = slice(KEY_AT[kv_head], KEY_AT[kv_head] + HEAD)
            value_at = slice(VALUE_AT[kv_head], VALUE_AT[kv_head] + HEAD)
            keys = window[micro, :, key_at]
            values = window[micro, :, value_at]
            queries = stacked_heads(query, micro, rows, kv_head)
            coming = stacked_heads(grad_attended, micro, rows, kv_head)
            shares = shares_of(queries, keys, bias[micro])
            grad_shares = against(coming, values)
            inner = jnp.sum(shares * grad_shares, axis=-1, keepdims=True)
            grad_scores = (shares * (grad_shares - inner)).astype(jnp.bfloat16)
            got = jnp.dot(grad_scores, keys, preferred_element_type=jnp.float32) * HEAD ** (-0.5)
            for number in range(group):
                head = kv_head * group + number
                grad_query[here, head * HEAD : (head + 1) * HEAD] = got[
                    number * rows : (number + 1) * rows, :
                ]
            grad_keys = across(grad_scores, queries) * HEAD ** (-0.5)
            grad_values = across(shares.astype(jnp.bfloat16), coming)
            for lane_at, item in ((key_at, grad_keys), (value_at, grad_values)):
                grad_two[here, lane_at] = item[:rows].astype(jnp.bfloat16)
                grad_one[here, lane_at] = item[rows : 2 * rows].astype(jnp.bfloat16)
                grad_own[here, lane_at] = item[2 * rows :]


def close_kernel(
    states_ref,
    grad_query,
    grad_own,
    got_one,
    got_two,
    grad_mixed,
    cosine,
    sine,
    gain,
    joined,
    grad_states,
    grad_joined,
    *refs,
):
    pair = (
        grad_own[...]
        + got_one[...].astype(jnp.float32)
        + got_two[...].astype(jnp.float32)
    )
    low = lane_low(pair.shape[0])
    tail = swap_halves(lanes(pair, 2))
    blocks = [grad_query[:, number * LANES : (number + 1) * LANES] for number in range(5)]
    blocks[4] = jnp.where(low, blocks[4], tail)
    blocks.append(lanes(pair, 0))
    back = -sine[...]
    blocks = [turned(block, cosine[...], back) for block in blocks]
    blocks.append(lanes(pair, 1))
    blocks.append(jnp.where(low, tail, 0.0))
    for number, block in enumerate(blocks):
        grad_joined[:, number * LANES : (number + 1) * LANES] = block.astype(jnp.bfloat16)
    grad_normed = against(grad_joined[...], joined[...])
    states = states_ref[...].astype(jnp.float32)
    scale = rms_scale(states)
    for gain_grad in refs:
        gain_grad[...] = jnp.broadcast_to(
            jnp.sum(states * scale * grad_normed, axis=0, keepdims=True), gain_grad.shape
        )
    grad_states[...] = (
        grad_mixed[...] + rms_back(states, scale, gain[0:1, :], grad_normed)
    ).astype(jnp.bfloat16)


def on_core(kernel, shapes, scratch, *operands):
    return pl.pallas_call(
        kernel,
        out_shape=tuple(jax.ShapeDtypeStruct(shape, dtype) for shape, dtype in shapes),
        in_specs=in_vmem(len(operands)),
        out_specs=tuple(in_vmem(len(shapes))),
        scratch_shapes=scratch,
        compiler_params=pltpu.CompilerParams(vmem_limit_bytes=VMEM_LIMIT),
        cost_estimate=pl.CostEstimate(flops=6_000_000_000, bytes_accessed=0, transcendentals=0),
    )(*operands)


def layer_forward(states, mats, gain_pair, tables, keep):
    joined, w_out, w_gate, w_up, w_down = mats
    cosine, sine, bias = tables
    rows = states.shape[0]
    low, wide = jnp.bfloat16, jnp.float32
    normed, query, pair = on_core(
        project_kernel,
        [((rows, D), low), ((rows, KEY_MAIN), low), ((rows, 3 * LANES), low)],
        [],
        states,
        gain_pair,
        joined,
        cosine,
        sine,
    )
    window = (passed_along(pair, "fsdp", 2), passed_along(pair, "fsdp", 1), pair)
    window_space = pltpu.VMEM((bias.shape[0], bias.shape[2], 3 * LANES), low)
    shapes = [
        ((rows, D), low),
        ((rows, D), low),
        ((rows, D), wide),
        ((rows, D), low),
        ((rows, FF), wide),
        ((rows, FF), wide),
        ((rows, FF), low),
    ]
    spaces = [pltpu.VMEM(*shapes[number]) for number in (1, 2, 6)]
    output, *kept = on_core(
        forward_kernel,
        shapes if keep else shapes[:1],
        [window_space] if keep else spaces + [window_space],
        states,
        query,
        *window,
        bias,
        gain_pair,
        w_out,
        w_gate,
        w_up,
        w_down,
    )
    return output, (normed, query, window, *kept)


def layer_backward(grad_output, states, kept, mats, gain_pair, tables, keep):
    joined, w_out, w_gate, w_up, w_down = mats
    cosine, sine, bias = tables
    normed, query, window, attended, mixed, normed_two, gate, up, hidden = kept
    rows = states.shape[0]
    low, wide = jnp.bfloat16, jnp.float32
    pair_shape = (rows, 3 * LANES)
    shapes = [
        ((rows, D), wide),
        ((rows, KEY_MAIN), wide),
        (pair_shape, low),
        (pair_shape, low),
        (pair_shape, wide),
    ]
    more = [((rows, FF), low), ((rows, FF), low), ((rows, D), low), ((8, D), wide)]
    spaces = [
        pltpu.VMEM((bias.shape[0], bias.shape[2], 3 * LANES), low),
        pltpu.VMEM((rows, D), low),
    ]
    if not keep:
        spaces = [pltpu.VMEM(*shape) for shape in more[:2]] + spaces
    grad_mixed, grad_query, grad_two, grad_one, grad_own, *record = on_core(
        backward_kernel,
        shapes + more if keep else shapes,
        spaces,
        grad_output,
        query,
        *window,
        bias,
        gain_pair,
        mixed,
        gate,
        up,
        w_out,
        w_gate,
        w_up,
        w_down,
    )
    got_one = passed_along(grad_one, "fsdp", -1)
    got_two = passed_along(grad_two, "fsdp", -2)
    halves = None
    if keep and lax.axis_size("fsdp") == 16:
        halves = wide_terms(
            block_index(REDUCE_ORDERS, False),
            (attended, normed_two, hidden, record[2], record[0], record[1], grad_output),
        )
    operands = (
        states,
        grad_query,
        grad_own,
        got_one,
        got_two,
        grad_mixed,
        cosine,
        sine,
        gain_pair,
        joined,
    )
    if not keep:
        return on_core(
            close_kernel, [((rows, D), low)], [pltpu.VMEM((rows, SLOTS), low)], *operands
        )[0]
    grad_states, grad_joined, gain_one = on_core(
        close_kernel, [((rows, D), low), ((rows, SLOTS), low), ((8, D), wide)], [], *operands
    )
    grad_gate, grad_up, grad_mixed_low, gain_two = record
    factors = (
        normed,
        attended,
        normed_two,
        hidden,
        grad_joined,
        grad_mixed_low,
        grad_gate,
        grad_up,
        grad_output,
    )
    return grad_states, factors, jnp.concatenate([gain_one[0], gain_two[0]]), halves


def local(ends, weights, gains, segments):
    micro_count = ends.shape[1]
    rows = ends.shape[2]
    first = lax.axis_index("section") == 0
    mats, gain_pair, segments = gather_layer(weights, gains, segments)
    marked = segments + 1
    rims = [passed_along(marked, "fsdp", 2), passed_along(marked, "fsdp", 1), marked]
    window_segments = jnp.concatenate(rims, axis=1)
    span = window_segments.shape[1]
    place = jnp.arange(span, dtype=jnp.int32)
    change = jnp.concatenate(
        [jnp.ones((micro_count, 1), dtype=bool), window_segments[:, 1:] != window_segments[:, :-1]],
        axis=1,
    )
    starts = lax.cummax(jnp.where(change, place[None, :], 0), axis=1)
    positions = (place[None, :] - starts)[:, span - rows :].reshape(-1)
    cosine, sine = rope_tables(positions)
    cosine = jnp.concatenate([cosine] * 4, axis=1)
    sine = jnp.concatenate([-sine, sine, -sine, sine], axis=1)
    allowed = (window_segments[:, span - rows :, None] == window_segments[:, None, :]) & (
        place[None, None, :] <= place[None, span - rows :, None]
    )
    bias = jnp.where(allowed, 0.0, masked_score).astype(jnp.float32)
    tables = (cosine, sine, bias)
    own = ends[0].reshape(micro_count * rows, D)
    middle, _ = layer_forward(own, mats, gain_pair, tables, False)
    states = jnp.where(first, own, passed_along(middle, "section", 1))
    output, kept = layer_forward(states, mats, gain_pair, tables, True)
    grad_middle = layer_backward(own, states, kept, mats, gain_pair, tables, False)
    grad_output = jnp.where(first, passed_along(grad_middle, "section", -1), own)
    grad_states, factors, gain_grad, halves = layer_backward(
        grad_output, states, kept, mats, gain_pair, tables, True
    )
    weight_share, gain_share = reduce_terms(factors, gain_grad, halves)
    ends_out = jnp.where(first, grad_states, output).reshape(ends.shape)
    return (ends_out, weight_share[None], gain_share[None])


def solution(mesh):
    placed = (
        P("section", None, "fsdp", None),
        P("section", "fsdp"),
        P("section", "fsdp"),
        P(None, "fsdp"),
    )
    return jax.shard_map(
        local,
        mesh=mesh,
        in_specs=placed,
        out_specs=(P("section", None, "fsdp", None), P("section", "fsdp"), P("section", "fsdp")),
        check_vma=False,
    )
```

```python
import jax
import jax.numpy as jnp
from jax import lax
from jax.experimental import pallas as pl
from jax.experimental.pallas import tpu as pltpu
from jax.sharding import PartitionSpec as P

D = 576
HEADS = 9
KV_HEADS = 3
HEAD = 64
FF = 1536
REACH = 2


epsilon = 1e-05
rope_base = 100000.0
masked_score = -1e30


def passed_along(value, axis, steps):
    count = lax.axis_size(axis)
    first, last = (max(0, -steps), min(count, count - steps))
    return lax.ppermute(value, axis, [(source, source + steps) for source in range(first, last)])


def rope_tables(positions):
    half = HEAD // 2
    frequency = rope_base ** (-2.0 * jnp.arange(half, dtype=jnp.float32) / HEAD)
    angles = positions.astype(jnp.float32)[:, None] * frequency[None, :]
    return (jnp.cos(angles), jnp.sin(angles))


def rms_scale(states):
    return lax.rsqrt(jnp.mean(states * states, axis=-1, keepdims=True) + epsilon)


def rms_back(states, scale, gain, grad):
    weighted = grad * gain
    return scale * weighted - states * (scale * scale * scale) * jnp.mean(
        weighted * states, axis=-1, keepdims=True
    )


def unpack(flat_vector):
    query_cols = HEADS * HEAD
    kv_cols = KV_HEADS * HEAD
    shapes = [
        (D, query_cols),
        (D, kv_cols),
        (D, kv_cols),
        (query_cols, D),
        (D, FF),
        (D, FF),
        (FF, D),
    ]
    pieces = []
    offset = 0
    for row_count, col_count in shapes:
        pieces.append(
            flat_vector[offset : offset + row_count * col_count].reshape(row_count, col_count)
        )
        offset = offset + row_count * col_count
    return pieces


LANES = 128
SHARD_ROWS = 1728
GAIN_ROWS = 16
BLOCK_ROWS = SHARD_ROWS + GAIN_ROWS
PIECE_ROWS = 864
VMEM_LIMIT = 20 * 1024 * 1024


def lane_low(rows):
    return lax.broadcasted_iota(jnp.int32, (rows, LANES), 1) < 64


def swap_halves(value):
    return pltpu.roll(value, 64, 1)


def narrow_pack(wide, natural, out_ref, start, columns):
    full = columns // LANES
    period = 2 * full + 1
    pairs = PIECE_ROWS // period
    low = lane_low(pairs)
    part = [wide[pl.ds(start + j, pairs, stride=period), :] for j in range(period)]
    at = start
    for c in range(full):
        natural[pl.ds(0, pairs, stride=2), :] = part[c]
        natural[pl.ds(1, pairs, stride=2), :] = swap_halves(
            jnp.where(low, part[full + c + 1], part[full + c])
        )
        out_ref[at : at + 2 * pairs, :] = natural[0 : 2 * pairs, :].astype(jnp.bfloat16)
        at += 2 * pairs
    natural[pl.ds(0, pairs, stride=2), :] = part[full]
    natural[pl.ds(1, pairs, stride=2), :] = swap_halves(part[2 * full])
    out_ref[at : at + pairs, :] = jnp.where(
        low, natural[0:pairs, :], swap_halves(natural[pairs : 2 * pairs, :])
    ).astype(jnp.bfloat16)


def narrow_unpack(packed, natural, out_ref, start, columns):
    full = columns // LANES
    period = 2 * full + 1
    pairs = PIECE_ROWS // period
    low = lane_low(pairs)
    evens, odds = [], []
    at = start
    for c in range(full):
        natural[0 : 2 * pairs, :] = packed[at : at + 2 * pairs, :]
        evens.append(natural[pl.ds(0, pairs, stride=2), :])
        odds.append(swap_halves(natural[pl.ds(1, pairs, stride=2), :]))
        at += 2 * pairs
    tail = packed[at : at + pairs, :]
    natural[0:pairs, :] = tail
    natural[pairs : 2 * pairs, :] = swap_halves(tail)
    tail_even = natural[pl.ds(0, pairs, stride=2), :]
    tail_odd = swap_halves(natural[pl.ds(1, pairs, stride=2), :])
    rows = evens + [jnp.where(low, tail_even, odds[0])]
    for c in range(full - 1):
        rows.append(jnp.where(low, odds[c], odds[c + 1]))
    rows.append(jnp.where(low, odds[full - 1], tail_odd))
    for j in range(period):
        out_ref[pl.ds(start + j, pairs, stride=period), :] = rows[j]


def by_owner(owner, narrow, wide):
    @pl.when((owner == 0) | (owner == 3) | (owner >= 12))
    def _():
        narrow(0, D)
        narrow(PIECE_ROWS, D)

    @pl.when(owner == 1)
    def _():
        narrow(0, D)
        narrow(PIECE_ROWS, KV_HEADS * HEAD)

    @pl.when(owner == 2)
    def _():
        narrow(0, KV_HEADS * HEAD)
        narrow(PIECE_ROWS, D)

    @pl.when((owner >= 4) & (owner < 12))
    def _():
        wide()


def pack_kernel(owner_ref, flat_ref, gain_ref, *refs):
    count = len(GATHER_CUTS) - 1
    chunks = refs[:count]
    wide, natural, block = refs[count:]
    for number in range(SHARD_ROWS):
        wide[number : number + 1, :] = flat_ref[
            0:1, number * LANES : (number + 1) * LANES
        ].astype(jnp.float32)
    block[SHARD_ROWS:BLOCK_ROWS, :] = gain_ref[...]

    def narrow(start, columns):
        narrow_pack(wide, natural, block, start, columns)

    def broad():
        blocks = FF // LANES
        rows = SHARD_ROWS // blocks
        for c in range(blocks):
            block[c * rows : (c + 1) * rows, :] = wide[pl.ds(c, rows, stride=blocks), :].astype(
                jnp.bfloat16
            )

    by_owner(owner_ref[0], narrow, broad)
    for number in range(count):
        chunks[number][...] = block[GATHER_CUTS[number] : GATHER_CUTS[number + 1], :]


def pack_shard(owner, flat, gain_rows):
    sizes = [GATHER_CUTS[n + 1] - GATHER_CUTS[n] for n in range(len(GATHER_CUTS) - 1)]
    return pl.pallas_call(
        pack_kernel,
        out_shape=tuple(jax.ShapeDtypeStruct((size, LANES), jnp.bfloat16) for size in sizes),
        in_specs=[pl.BlockSpec(memory_space=pltpu.SMEM)] + in_vmem(2),
        out_specs=tuple(in_vmem(len(sizes))),
        scratch_shapes=[
            pltpu.VMEM((SHARD_ROWS, LANES), jnp.float32),
            pltpu.VMEM((1152, LANES), jnp.float32),
            pltpu.VMEM((BLOCK_ROWS, LANES), jnp.bfloat16),
        ],
        compiler_params=pltpu.CompilerParams(vmem_limit_bytes=VMEM_LIMIT),
        cost_estimate=pl.CostEstimate(flops=6_000_000_000, bytes_accessed=0, transcendentals=0),
    )(owner, flat, gain_rows)


def finish_kernel(owner_ref, *refs):
    count = len(REDUCE_CUTS) - 1
    kept_refs, got_refs = refs[:count], refs[count : 2 * count]
    out_ref, gain_ref, total, natural = refs[2 * count :]
    for number in range(count):
        total[REDUCE_CUTS[number] : REDUCE_CUTS[number + 1], :] = kept_refs[number][
            ...
        ].astype(jnp.float32) + got_refs[number][...].astype(jnp.float32)
    gain_ref[...] = total[SHARD_ROWS:, :]

    def narrow(start, columns):
        narrow_unpack(total, natural, out_ref, start, columns)

    def broad():
        blocks = FF // LANES
        rows = SHARD_ROWS // blocks
        for c in range(blocks):
            out_ref[pl.ds(c, rows, stride=blocks), :] = total[c * rows : (c + 1) * rows, :]

    by_owner(owner_ref[0], narrow, broad)


def in_vmem(count):
    return [pl.BlockSpec(memory_space=pltpu.VMEM)] * count


def finish_shard(owner, kept, got):
    return pl.pallas_call(
        finish_kernel,
        out_shape=(
            jax.ShapeDtypeStruct((SHARD_ROWS, LANES), jnp.float32),
            jax.ShapeDtypeStruct((GAIN_ROWS, LANES), jnp.float32),
        ),
        in_specs=[pl.BlockSpec(memory_space=pltpu.SMEM)] + in_vmem(len(kept) + len(got)),
        out_specs=tuple(in_vmem(2)),
        scratch_shapes=[
            pltpu.VMEM((BLOCK_ROWS, LANES), jnp.float32),
            pltpu.VMEM((1152, LANES), jnp.float32),
        ],
        compiler_params=pltpu.CompilerParams(vmem_limit_bytes=VMEM_LIMIT),
        cost_estimate=pl.CostEstimate(flops=6_000_000_000, bytes_accessed=0, transcendentals=0),
    )(owner, *kept, *got)


SLOTS = 1024
KEY_MAIN = 640
KEY_TAIL = 576
VALUE_MAIN = 768
VALUE_TAIL = 896
GATHER_CUTS = (0, 544, 1088, 1408, 1744)
GATHER_ORDERS = ((8, 4, 2, 1), (4, 8, 1, 2), (2, 1, 8, 4), (1, 2, 4, 8))
REDUCE_CUTS = (0, 320, 640, 1088, 1408, 1744)
REDUCE_ORDERS = (
    (1, 2, 4, 8),
    (2, 1, 4, 8),
    (4, 8, 1, 2),
    (1, 2, 4, 8),
    (2, 1, 4, 8),
)


def place_narrow(block, at, target, row, main, tail, columns):
    full = columns // LANES
    pairs = PIECE_ROWS // (2 * full + 1)
    for c in range(full):
        target[pl.ds(row, 2 * pairs), main + c * LANES : main + (c + 1) * LANES] = block[
            at : at + 2 * pairs, :
        ]
        at += 2 * pairs
    target[pl.ds(row, pairs), tail : tail + 64] = block[at : at + pairs, :64]
    target[pl.ds(row + pairs, pairs), tail : tail + 64] = block[at : at + pairs, 64:]


def place_kernel(index_ref, *refs):
    count = len(GATHER_CUTS) - 1
    chunks = refs[:count]
    joined, out, gate, up, down, gain, block = refs[count:]
    owner = pl.program_id(0)
    kv_width = KV_HEADS * HEAD
    for number in range(count):
        block[GATHER_CUTS[number] : GATHER_CUTS[number + 1], :] = chunks[number][
            index_ref[number, owner]
        ]
    gain[pl.ds(pl.multiple_of(owner * GAIN_ROWS, GAIN_ROWS), GAIN_ROWS), :] = block[SHARD_ROWS:, :]

    @pl.when(owner == 0)
    def _():
        joined[:, SLOTS - 128 :] = jnp.zeros((D, 128), jnp.bfloat16)
        place_narrow(block, 0, joined, 0, 0, 512, D)
        place_narrow(block, PIECE_ROWS, joined, 192, 0, 512, D)

    @pl.when(owner == 1)
    def _():
        place_narrow(block, 0, joined, 384, 0, 512, D)
        place_narrow(block, PIECE_ROWS, joined, 0, KEY_MAIN, KEY_TAIL, kv_width)

    @pl.when(owner == 2)
    def _():
        place_narrow(block, 0, joined, 0, VALUE_MAIN, VALUE_TAIL, kv_width)
        place_narrow(block, PIECE_ROWS, out, 0, 0, 512, D)

    @pl.when(owner == 3)
    def _():
        place_narrow(block, 0, out, 192, 0, 512, D)
        place_narrow(block, PIECE_ROWS, out, 384, 0, 512, D)

    def broad(target, first):
        @pl.when((owner >= first) & (owner < first + 4))
        def _():
            row = pl.multiple_of((owner - first) * 144, 16)
            for c in range(FF // LANES):
                target[pl.ds(row, 144), c * LANES : (c + 1) * LANES] = block[
                    c * 144 : (c + 1) * 144, :
                ]

    broad(gate, 4)
    broad(up, 8)

    @pl.when(owner >= 12)
    def _():
        row = pl.multiple_of((owner - 12) * 384, 16)
        place_narrow(block, 0, down, row, 0, 512, D)
        place_narrow(block, PIECE_ROWS, down, pl.multiple_of(row + 192, 16), 0, 512, D)


def place_blocks(index, chunks):
    shapes = [(D, SLOTS), (D, D), (D, FF), (D, FF), (FF, D), (16 * GAIN_ROWS, LANES)]
    return pl.pallas_call(
        place_kernel,
        out_shape=tuple(jax.ShapeDtypeStruct(shape, jnp.bfloat16) for shape in shapes),
        grid=(16,),
        in_specs=[pl.BlockSpec(memory_space=pltpu.SMEM)] + in_vmem(len(chunks)),
        out_specs=tuple(in_vmem(len(shapes))),
        scratch_shapes=[pltpu.VMEM((BLOCK_ROWS, LANES), jnp.bfloat16)],
        compiler_params=pltpu.CompilerParams(vmem_limit_bytes=VMEM_LIMIT),
        cost_estimate=pl.CostEstimate(flops=6_000_000_000, bytes_accessed=0, transcendentals=0),
    )(index, *chunks)


def store_narrow(result, block, at, main, tail, columns):
    full = columns // LANES
    pairs = PIECE_ROWS // (2 * full + 1)
    for c in range(full):
        block[at : at + 2 * pairs, :] = result[
            :, main + c * LANES : main + (c + 1) * LANES
        ].astype(jnp.bfloat16)
        at += 2 * pairs
    block[at : at + pairs, :] = jnp.concatenate(
        [result[:pairs, tail : tail + 64], result[pairs:, tail : tail + 64]], axis=1
    ).astype(jnp.bfloat16)


def deal_block(index_ref, halves, block, owner):
    for number in range(len(REDUCE_CUTS) - 1):
        first, last = REDUCE_CUTS[number], REDUCE_CUTS[number + 1]
        place = index_ref[number, owner]

        @pl.when(place < 8)
        def _():
            halves[2 * number][place] = block[first:last, :]

        @pl.when(place >= 8)
        def _():
            halves[2 * number + 1][place - 8] = block[first:last, :]


def turned_product(turned_ref, row, count, right):
    return jnp.dot(turned_ref[row : row + count, :], right, preferred_element_type=jnp.float32)


def wide_terms_kernel(
    attended,
    normed_two,
    hidden,
    grad_mixed,
    grad_gate,
    grad_up,
    grad_output,
    blocks,
    attended_t,
    normed_two_t,
    hidden_t,
):
    normed_two_t[...] = normed_two[...].T
    for number, right in ((0, grad_gate), (1, grad_up)):
        for part in range(4):
            result = turned_product(normed_two_t, 144 * part, 144, right[...]).astype(jnp.bfloat16)
            for c in range(FF // LANES):
                blocks[1 + 4 * number + part, c * 144 : (c + 1) * 144, :] = lanes(result, c)
    hidden_t[...] = hidden[...].T
    for part in range(4):
        block = blocks.at[9 + part]
        for half in range(2):
            result = turned_product(hidden_t, 384 * part + 192 * half, 192, grad_output[...])
            store_narrow(result, block, half * PIECE_ROWS, 0, 512, D)
    attended_t[...] = attended[...].T
    block = blocks.at[0]
    for half in range(2):
        result = turned_product(attended_t, 192 + 192 * half, 192, grad_mixed[...])
        store_narrow(result, block, half * PIECE_ROWS, 0, 512, D)


def narrow_terms_kernel(index_ref, normed, attended, grad_joined, grad_mixed, gain_ref, *refs):
    wide_blocks = refs[0]
    *halves, block, normed_t, attended_t = refs[1:]
    kv_width = KV_HEADS * HEAD
    normed_t[...] = normed[...].T
    attended_t[...] = attended[...].T
    query = grad_joined[:, :KEY_MAIN]
    for owner in range(16):
        block[SHARD_ROWS:BLOCK_ROWS, :] = gain_ref[owner]
        if owner == 0:
            for half in range(2):
                result = turned_product(normed_t, 192 * half, 192, query)
                store_narrow(result, block, half * PIECE_ROWS, 0, 512, D)
        elif owner == 1:
            store_narrow(turned_product(normed_t, 384, 192, query), block, 0, 0, 512, D)
            key = turned_product(normed_t, 0, D, grad_joined[:, 512:768])
            store_narrow(key, block, PIECE_ROWS, KEY_MAIN - 512, KEY_TAIL - 512, kv_width)
        elif owner == 2:
            value = turned_product(normed_t, 0, D, grad_joined[:, VALUE_MAIN:])
            store_narrow(value, block, 0, 0, VALUE_TAIL - VALUE_MAIN, kv_width)
            result = turned_product(attended_t, 0, 192, grad_mixed[...])
            store_narrow(result, block, PIECE_ROWS, 0, 512, D)
        else:
            block[:SHARD_ROWS, :] = wide_blocks[owner - 3]
        deal_block(index_ref, halves, block, owner)


def wide_terms(factors):
    rows = factors[0].shape[0]
    return on_core(
        wide_terms_kernel,
        [((13, SHARD_ROWS, LANES), jnp.bfloat16)],
        [
            pltpu.VMEM((D, rows), jnp.bfloat16),
            pltpu.VMEM((D, rows), jnp.bfloat16),
            pltpu.VMEM((FF, rows), jnp.bfloat16),
        ],
        *factors,
    )[0]


def narrow_terms(index, factors, gain_rows, wide_blocks):
    shapes = tuple(
        jax.ShapeDtypeStruct((8, REDUCE_CUTS[n + 1] - REDUCE_CUTS[n], LANES), jnp.bfloat16)
        for n in range(len(REDUCE_CUTS) - 1)
        for _ in range(2)
    )
    rows = factors[0].shape[0]
    return pl.pallas_call(
        narrow_terms_kernel,
        out_shape=shapes,
        in_specs=[pl.BlockSpec(memory_space=pltpu.SMEM)] + in_vmem(len(factors) + 2),
        out_specs=tuple(in_vmem(len(shapes))),
        scratch_shapes=[
            pltpu.VMEM((BLOCK_ROWS, LANES), jnp.bfloat16),
            pltpu.VMEM((D, rows), jnp.bfloat16),
            pltpu.VMEM((D, rows), jnp.bfloat16),
        ],
        compiler_params=pltpu.CompilerParams(vmem_limit_bytes=VMEM_LIMIT),
        cost_estimate=pl.CostEstimate(flops=6_000_000_000, bytes_accessed=0, transcendentals=0),
    )(index, *factors, gain_rows, wide_blocks)


def partner(value, stride):
    count = lax.axis_size("fsdp")
    return lax.ppermute(value, "fsdp", [(source, source ^ stride) for source in range(count)])


def block_index(orders, first_is_low):
    apart = jnp.arange(16, dtype=jnp.int32) ^ lax.axis_index("fsdp").astype(jnp.int32)
    rows = []
    for order in orders:
        place = jnp.zeros_like(apart)
        for stage, stride in enumerate(order):
            bit = stage if first_is_low else len(order) - 1 - stage
            place = place + jnp.where((apart & stride) != 0, 1 << bit, 0)
        rows.append(place)
    return jnp.stack(rows)


def gather_layer(weights, gains, segments):
    owners = lax.axis_size("fsdp")
    if owners != 16:
        flat_full = lax.all_gather(weights[0], "fsdp", axis=0, tiled=True)
        gain_full = lax.all_gather(gains[0], "fsdp", axis=0, tiled=True)
        query, key, value, out, gate, up, down = unpack(flat_full)
        joined = jnp.concatenate(
            [
                query,
                key[:, LANES:],
                key[:, :LANES],
                value,
                jnp.zeros((D, SLOTS - VALUE_TAIL - 64), jnp.bfloat16),
            ],
            axis=1,
        )
        return (joined, out, gate, up, down), gain_full.astype(jnp.float32).reshape(2, D), segments
    owner = lax.axis_index("fsdp").astype(jnp.int32).reshape(1)
    share = gains.shape[1]
    gain_rows = jnp.pad(gains, ((0, GAIN_ROWS - 1), (0, LANES - share)))
    chunks = list(pack_shard(owner, weights, gain_rows))
    segments, *chunks = lax.optimization_barrier((segments, *chunks))
    for stage in range(4):
        got = [partner(chunk, order[stage]) for chunk, order in zip(chunks, GATHER_ORDERS)]
        chunks = [jnp.concatenate(both) for both in zip(chunks, got)]
    chunks = [chunk.reshape(16, -1, LANES) for chunk in chunks]
    *mats, gain_full = place_blocks(block_index(GATHER_ORDERS, True), chunks)
    gain_full = gain_full.reshape(16, GAIN_ROWS, LANES)[:, 0, :share]
    return tuple(mats), gain_full.astype(jnp.float32).reshape(2, D), segments


def reduce_terms(factors, gain_grad, wide_blocks):
    owners = lax.axis_size("fsdp")
    share = gain_grad.shape[0] // owners
    if owners != 16:
        normed, attended, normed_two, hidden, joined, grad_mixed, grad_gate, grad_up, last = factors
        pairs = [
            (normed, joined[:, :D]),
            (normed, jnp.concatenate([joined[:, KEY_MAIN:VALUE_MAIN], joined[:, D:KEY_MAIN]], 1)),
            (normed, joined[:, VALUE_MAIN : VALUE_TAIL + 64]),
            (attended, grad_mixed),
            (normed_two, grad_gate),
            (normed_two, grad_up),
            (hidden, last),
        ]
        flat_grads = jnp.concatenate(
            [
                jnp.einsum("rd,re->de", left, right, preferred_element_type=jnp.float32).reshape(-1)
                for left, right in pairs
            ]
        )
        got = [
            lax.all_to_all(
                item.reshape(owners, -1).astype(jnp.bfloat16),
                "fsdp",
                split_axis=0,
                concat_axis=0,
                tiled=True,
            ).astype(jnp.float32)
            for item in (flat_grads, gain_grad)
        ]
        return tuple(jnp.sum(item, axis=0) for item in got)
    gain_rows = jnp.pad(
        gain_grad.reshape(owners, 1, share).astype(jnp.bfloat16),
        ((0, 0), (0, GAIN_ROWS - 1), (0, LANES - share)),
    )
    normed, attended, _, _, grad_joined, grad_mixed = factors[:6]
    halves = narrow_terms(
        block_index(REDUCE_ORDERS, False),
        (normed, attended, grad_joined, grad_mixed),
        gain_rows,
        wide_blocks,
    )
    kept, sent = halves[0::2], halves[1::2]
    for stage in range(4):
        if stage:
            half = 8 >> stage
            kept, sent = [item[:half] for item in sums], [item[half:] for item in sums]
        got = [partner(item, order[stage]) for item, order in zip(sent, REDUCE_ORDERS)]
        if stage < 3:
            sums = [
                (one.astype(jnp.float32) + other.astype(jnp.float32)).astype(jnp.bfloat16)
                for one, other in zip(kept, got)
            ]
    owner = lax.axis_index("fsdp").astype(jnp.int32).reshape(1)
    flat, gain = finish_shard(owner, [item[0] for item in kept], [item[0] for item in got])
    return flat.reshape(-1), gain[0, :share]


def turned(block, cosine, sine):
    low = lax.broadcasted_iota(jnp.int32, block.shape, 1) % 64 < 32
    other = jnp.where(low, pltpu.roll(block, 96, 1), pltpu.roll(block, 32, 1))
    return block * cosine + other * sine


def lanes(value, number):
    return value[:, number * LANES : (number + 1) * LANES]


def project_kernel(states_ref, gain, joined, cosine, sine, normed, query, pair):
    states = states_ref[...].astype(jnp.float32)
    low_rows = (states * rms_scale(states) * gain[0:1, :]).astype(jnp.bfloat16)
    normed[...] = low_rows
    full = jnp.dot(low_rows, joined[...], preferred_element_type=jnp.float32)
    blocks = [turned(lanes(full, number), cosine[...], sine[...]) for number in range(6)]
    for number in range(5):
        query[:, number * LANES : (number + 1) * LANES] = blocks[number].astype(jnp.bfloat16)
    low = lane_low(full.shape[0])
    pair[:, :LANES] = blocks[5].astype(jnp.bfloat16)
    pair[:, LANES : 2 * LANES] = lanes(full, 6).astype(jnp.bfloat16)
    pair[:, 2 * LANES :] = jnp.where(
        low, swap_halves(blocks[4]), swap_halves(lanes(full, 7))
    ).astype(jnp.bfloat16)


KEY_AT = (0, 64, 256)
VALUE_AT = (128, 192, 320)


def fill_window(window, pieces):
    micro_count, span, _ = window.shape
    rows = span // len(pieces)
    for micro in range(micro_count):
        for number, piece in enumerate(pieces):
            window[micro, number * rows : (number + 1) * rows, :] = piece[
                micro * rows : (micro + 1) * rows, :
            ]


def stacked_heads(ref, micro, rows, kv_head):
    group = HEADS // KV_HEADS
    return jnp.concatenate(
        [
            ref[micro * rows : (micro + 1) * rows, head * HEAD : (head + 1) * HEAD]
            for head in range(kv_head * group, (kv_head + 1) * group)
        ],
        axis=0,
    )


def shares_of(queries, keys, bias):
    scores = lax.dot_general(
        queries, keys, (((1,), (1,)), ((), ())), preferred_element_type=jnp.float32
    ) * HEAD ** (-0.5)
    group = HEADS // KV_HEADS
    rows, span = bias.shape
    scores = scores.reshape(group, rows, span) + bias[None]
    powers = jnp.exp(scores - jnp.max(scores, axis=-1, keepdims=True))
    shares = powers / jnp.sum(powers, axis=-1, keepdims=True)
    return shares.reshape(group * rows, span)


def forward_kernel(
    states,
    query,
    pair_two,
    pair_one,
    pair_own,
    bias,
    gain,
    w_out,
    w_gate,
    w_up,
    w_down,
    output,
    *refs,
):
    if len(refs) == 7:
        attended, mixed, normed_two, gate, up, hidden, window = refs
    else:
        attended, mixed, hidden, window = refs
        normed_two = gate = up = None
    group = HEADS // KV_HEADS
    fill_window(window, (pair_two, pair_one, pair_own))
    micro_count, rows, _ = bias.shape
    for micro in range(micro_count):
        for kv_head in range(KV_HEADS):
            keys = window[micro, :, KEY_AT[kv_head] : KEY_AT[kv_head] + HEAD]
            values = window[micro, :, VALUE_AT[kv_head] : VALUE_AT[kv_head] + HEAD]
            shares = shares_of(stacked_heads(query, micro, rows, kv_head), keys, bias[micro])
            got = jnp.dot(
                shares.astype(jnp.bfloat16), values, preferred_element_type=jnp.float32
            ).astype(jnp.bfloat16)
            for number in range(group):
                head = kv_head * group + number
                attended[micro * rows : (micro + 1) * rows, head * HEAD : (head + 1) * HEAD] = got[
                    number * rows : (number + 1) * rows, :
                ]
    middle = states[...].astype(jnp.float32) + jnp.dot(
        attended[...], w_out[...], preferred_element_type=jnp.float32
    )
    mixed[...] = middle
    low_rows = (middle * rms_scale(middle) * gain[1:2, :]).astype(jnp.bfloat16)
    if normed_two is not None:
        normed_two[...] = low_rows
    width = FF // 3
    for part in range(3):
        at = slice(part * width, (part + 1) * width)
        gates = jnp.dot(low_rows, w_gate[:, at], preferred_element_type=jnp.float32)
        ups = jnp.dot(low_rows, w_up[:, at], preferred_element_type=jnp.float32)
        if gate is not None:
            gate[:, at] = gates
            up[:, at] = ups
        hidden[:, at] = (gates * jax.nn.sigmoid(gates) * ups).astype(jnp.bfloat16)
    output[...] = (
        mixed[...] + jnp.dot(hidden[...], w_down[...], preferred_element_type=jnp.float32)
    ).astype(jnp.bfloat16)


def against(left, right):
    return lax.dot_general(left, right, (((1,), (1,)), ((), ())), preferred_element_type=jnp.float32)


def across(left, right):
    return lax.dot_general(left, right, (((0,), (0,)), ((), ())), preferred_element_type=jnp.float32)


def backward_kernel(
    grad_output,
    query,
    pair_two,
    pair_one,
    pair_own,
    bias,
    gain,
    mixed,
    gate,
    up,
    w_out,
    w_gate,
    w_up,
    w_down,
    grad_mixed,
    grad_query,
    grad_two,
    grad_one,
    grad_own,
    *refs,
):
    if len(refs) == 6:
        grad_gate, grad_up, grad_mixed_low, gain_grad, window, grad_attended = refs
    else:
        grad_gate, grad_up, window, grad_attended = refs
        grad_mixed_low = gain_grad = None
    group = HEADS // KV_HEADS
    fill_window(window, (pair_two, pair_one, pair_own))
    width = FF // 3
    grads = grad_output[...]
    for part in range(3):
        at = slice(part * width, (part + 1) * width)
        grad_hidden = against(grads, w_down[at, :])
        gates = gate[:, at]
        sigmoid = jax.nn.sigmoid(gates)
        grad_gate[:, at] = (
            grad_hidden * up[:, at] * sigmoid * (1.0 + gates * (1.0 - sigmoid))
        ).astype(jnp.bfloat16)
        grad_up[:, at] = (grad_hidden * gates * sigmoid).astype(jnp.bfloat16)
    grad_normed = against(grad_gate[...], w_gate[...]) + against(grad_up[...], w_up[...])
    middle = mixed[...]
    scale = rms_scale(middle)
    if gain_grad is not None:
        gain_grad[...] = jnp.broadcast_to(
            jnp.sum(middle * scale * grad_normed, axis=0, keepdims=True), gain_grad.shape
        )
    grad_middle = grads.astype(jnp.float32) + rms_back(middle, scale, gain[1:2, :], grad_normed)
    grad_mixed[...] = grad_middle
    low_rows = grad_middle.astype(jnp.bfloat16)
    if grad_mixed_low is not None:
        grad_mixed_low[...] = low_rows
    grad_attended[...] = against(low_rows, w_out[...]).astype(jnp.bfloat16)
    micro_count, rows, _ = bias.shape
    for micro in range(micro_count):
        here = slice(micro * rows, (micro + 1) * rows)
        for kv_head in range(KV_HEADS):
            key_at = slice(KEY_AT[kv_head], KEY_AT[kv_head] + HEAD)
            value_at = slice(VALUE_AT[kv_head], VALUE_AT[kv_head] + HEAD)
            keys = window[micro, :, key_at]
            values = window[micro, :, value_at]
            queries = stacked_heads(query, micro, rows, kv_head)
            coming = stacked_heads(grad_attended, micro, rows, kv_head)
            shares = shares_of(queries, keys, bias[micro])
            grad_shares = against(coming, values)
            inner = jnp.sum(shares * grad_shares, axis=-1, keepdims=True)
            grad_scores = (shares * (grad_shares - inner)).astype(jnp.bfloat16)
            got = jnp.dot(grad_scores, keys, preferred_element_type=jnp.float32) * HEAD ** (-0.5)
            for number in range(group):
                head = kv_head * group + number
                grad_query[here, head * HEAD : (head + 1) * HEAD] = got[
                    number * rows : (number + 1) * rows, :
                ]
            grad_keys = across(grad_scores, queries) * HEAD ** (-0.5)
            grad_values = across(shares.astype(jnp.bfloat16), coming)
            for lane_at, item in ((key_at, grad_keys), (value_at, grad_values)):
                grad_two[here, lane_at] = item[:rows].astype(jnp.bfloat16)
                grad_one[here, lane_at] = item[rows : 2 * rows].astype(jnp.bfloat16)
                grad_own[here, lane_at] = item[2 * rows :]


def close_kernel(
    states_ref,
    grad_query,
    grad_own,
    got_one,
    got_two,
    grad_mixed,
    cosine,
    sine,
    gain,
    joined,
    grad_states,
    grad_joined,
    *refs,
):
    pair = (
        grad_own[...]
        + got_one[...].astype(jnp.float32)
        + got_two[...].astype(jnp.float32)
    )
    low = lane_low(pair.shape[0])
    tail = swap_halves(lanes(pair, 2))
    blocks = [grad_query[:, number * LANES : (number + 1) * LANES] for number in range(5)]
    blocks[4] = jnp.where(low, blocks[4], tail)
    blocks.append(lanes(pair, 0))
    back = -sine[...]
    blocks = [turned(block, cosine[...], back) for block in blocks]
    blocks.append(lanes(pair, 1))
    blocks.append(jnp.where(low, tail, 0.0))
    for number, block in enumerate(blocks):
        grad_joined[:, number * LANES : (number + 1) * LANES] = block.astype(jnp.bfloat16)
    grad_normed = against(grad_joined[...], joined[...])
    states = states_ref[...].astype(jnp.float32)
    scale = rms_scale(states)
    for gain_grad in refs:
        gain_grad[...] = jnp.broadcast_to(
            jnp.sum(states * scale * grad_normed, axis=0, keepdims=True), gain_grad.shape
        )
    grad_states[...] = (
        grad_mixed[...] + rms_back(states, scale, gain[0:1, :], grad_normed)
    ).astype(jnp.bfloat16)


def on_core(kernel, shapes, scratch, *operands):
    return pl.pallas_call(
        kernel,
        out_shape=tuple(jax.ShapeDtypeStruct(shape, dtype) for shape, dtype in shapes),
        in_specs=in_vmem(len(operands)),
        out_specs=tuple(in_vmem(len(shapes))),
        scratch_shapes=scratch,
        compiler_params=pltpu.CompilerParams(vmem_limit_bytes=VMEM_LIMIT),
        cost_estimate=pl.CostEstimate(flops=6_000_000_000, bytes_accessed=0, transcendentals=0),
    )(*operands)


def layer_forward(states, mats, gain_pair, tables, keep):
    joined, w_out, w_gate, w_up, w_down = mats
    cosine, sine, bias = tables
    rows = states.shape[0]
    low, wide = jnp.bfloat16, jnp.float32
    normed, query, pair = on_core(
        project_kernel,
        [((rows, D), low), ((rows, KEY_MAIN), low), ((rows, 3 * LANES), low)],
        [],
        states,
        gain_pair,
        joined,
        cosine,
        sine,
    )
    window = (passed_along(pair, "fsdp", 2), passed_along(pair, "fsdp", 1), pair)
    window_space = pltpu.VMEM((bias.shape[0], bias.shape[2], 3 * LANES), low)
    shapes = [
        ((rows, D), low),
        ((rows, D), low),
        ((rows, D), wide),
        ((rows, D), low),
        ((rows, FF), wide),
        ((rows, FF), wide),
        ((rows, FF), low),
    ]
    spaces = [pltpu.VMEM(*shapes[number]) for number in (1, 2, 6)]
    output, *kept = on_core(
        forward_kernel,
        shapes if keep else shapes[:1],
        [window_space] if keep else spaces + [window_space],
        states,
        query,
        *window,
        bias,
        gain_pair,
        w_out,
        w_gate,
        w_up,
        w_down,
    )
    return output, (normed, query, window, *kept)


def layer_backward(grad_output, states, kept, mats, gain_pair, tables, keep):
    joined, w_out, w_gate, w_up, w_down = mats
    cosine, sine, bias = tables
    normed, query, window, attended, mixed, normed_two, gate, up, hidden = kept
    rows = states.shape[0]
    low, wide = jnp.bfloat16, jnp.float32
    pair_shape = (rows, 3 * LANES)
    shapes = [
        ((rows, D), wide),
        ((rows, KEY_MAIN), wide),
        (pair_shape, low),
        (pair_shape, low),
        (pair_shape, wide),
    ]
    more = [((rows, FF), low), ((rows, FF), low), ((rows, D), low), ((8, D), wide)]
    spaces = [
        pltpu.VMEM((bias.shape[0], bias.shape[2], 3 * LANES), low),
        pltpu.VMEM((rows, D), low),
    ]
    if not keep:
        spaces = [pltpu.VMEM(*shape) for shape in more[:2]] + spaces
    grad_mixed, grad_query, grad_two, grad_one, grad_own, *record = on_core(
        backward_kernel,
        shapes + more if keep else shapes,
        spaces,
        grad_output,
        query,
        *window,
        bias,
        gain_pair,
        mixed,
        gate,
        up,
        w_out,
        w_gate,
        w_up,
        w_down,
    )
    got_one = passed_along(grad_one, "fsdp", -1)
    got_two = passed_along(grad_two, "fsdp", -2)
    wide_blocks = None
    if keep and lax.axis_size("fsdp") == 16:
        wide_blocks = wide_terms(
            (attended, normed_two, hidden, record[2], record[0], record[1], grad_output)
        )
    operands = (
        states,
        grad_query,
        grad_own,
        got_one,
        got_two,
        grad_mixed,
        cosine,
        sine,
        gain_pair,
        joined,
    )
    if not keep:
        return on_core(
            close_kernel, [((rows, D), low)], [pltpu.VMEM((rows, SLOTS), low)], *operands
        )[0]
    grad_states, grad_joined, gain_one = on_core(
        close_kernel, [((rows, D), low), ((rows, SLOTS), low), ((8, D), wide)], [], *operands
    )
    grad_gate, grad_up, grad_mixed_low, gain_two = record
    factors = (
        normed,
        attended,
        normed_two,
        hidden,
        grad_joined,
        grad_mixed_low,
        grad_gate,
        grad_up,
        grad_output,
    )
    return grad_states, factors, jnp.concatenate([gain_one[0], gain_two[0]]), wide_blocks


def local(ends, weights, gains, segments):
    micro_count = ends.shape[1]
    rows = ends.shape[2]
    first = lax.axis_index("section") == 0
    mats, gain_pair, segments = gather_layer(weights, gains, segments)
    marked = segments + 1
    rims = [passed_along(marked, "fsdp", 2), passed_along(marked, "fsdp", 1), marked]
    window_segments = jnp.concatenate(rims, axis=1)
    span = window_segments.shape[1]
    place = jnp.arange(span, dtype=jnp.int32)
    change = jnp.concatenate(
        [jnp.ones((micro_count, 1), dtype=bool), window_segments[:, 1:] != window_segments[:, :-1]],
        axis=1,
    )
    starts = lax.cummax(jnp.where(change, place[None, :], 0), axis=1)
    positions = (place[None, :] - starts)[:, span - rows :].reshape(-1)
    cosine, sine = rope_tables(positions)
    cosine = jnp.concatenate([cosine] * 4, axis=1)
    sine = jnp.concatenate([-sine, sine, -sine, sine], axis=1)
    allowed = (window_segments[:, span - rows :, None] == window_segments[:, None, :]) & (
        place[None, None, :] <= place[None, span - rows :, None]
    )
    bias = jnp.where(allowed, 0.0, masked_score).astype(jnp.float32)
    tables = (cosine, sine, bias)
    own = ends[0].reshape(micro_count * rows, D)
    middle, _ = layer_forward(own, mats, gain_pair, tables, False)
    states = jnp.where(first, own, passed_along(middle, "section", 1))
    output, kept = layer_forward(states, mats, gain_pair, tables, True)
    grad_middle = layer_backward(own, states, kept, mats, gain_pair, tables, False)
    grad_output = jnp.where(first, passed_along(grad_middle, "section", -1), own)
    grad_states, factors, gain_grad, wide_blocks = layer_backward(
        grad_output, states, kept, mats, gain_pair, tables, True
    )
    weight_share, gain_share = reduce_terms(factors, gain_grad, wide_blocks)
    ends_out = jnp.where(first, grad_states, output).reshape(ends.shape)
    return (ends_out, weight_share[None], gain_share[None])


def solution(mesh):
    placed = (
        P("section", None, "fsdp", None),
        P("section", "fsdp"),
        P("section", "fsdp"),
        P(None, "fsdp"),
    )
    return jax.shard_map(
        local,
        mesh=mesh,
        in_specs=placed,
        out_specs=(P("section", None, "fsdp", None), P("section", "fsdp"), P("section", "fsdp")),
        check_vma=False,
    )
```

```python
import jax
import jax.numpy as jnp
from jax import lax
from jax.experimental import pallas as pl
from jax.experimental.pallas import tpu as pltpu
from jax.sharding import PartitionSpec as P

D = 576
HEADS = 9
KV_HEADS = 3
HEAD = 64
FF = 1536
REACH = 2


epsilon = 1e-05
rope_base = 100000.0
masked_score = -1e30


def passed_along(value, axis, steps):
    count = lax.axis_size(axis)
    first, last = (max(0, -steps), min(count, count - steps))
    return lax.ppermute(value, axis, [(source, source + steps) for source in range(first, last)])


def rope_tables(positions):
    half = HEAD // 2
    frequency = rope_base ** (-2.0 * jnp.arange(half, dtype=jnp.float32) / HEAD)
    angles = positions.astype(jnp.float32)[:, None] * frequency[None, :]
    return (jnp.cos(angles), jnp.sin(angles))


def rms_scale(states):
    return lax.rsqrt(jnp.mean(states * states, axis=-1, keepdims=True) + epsilon)


def rms_back(states, scale, gain, grad):
    weighted = grad * gain
    return scale * weighted - states * (scale * scale * scale) * jnp.mean(
        weighted * states, axis=-1, keepdims=True
    )


def unpack(flat_vector):
    query_cols = HEADS * HEAD
    kv_cols = KV_HEADS * HEAD
    shapes = [
        (D, query_cols),
        (D, kv_cols),
        (D, kv_cols),
        (query_cols, D),
        (D, FF),
        (D, FF),
        (FF, D),
    ]
    pieces = []
    offset = 0
    for row_count, col_count in shapes:
        pieces.append(
            flat_vector[offset : offset + row_count * col_count].reshape(row_count, col_count)
        )
        offset = offset + row_count * col_count
    return pieces


LANES = 128
SHARD_ROWS = 1728
GAIN_ROWS = 16
BLOCK_ROWS = SHARD_ROWS + GAIN_ROWS
PIECE_ROWS = 864
VMEM_LIMIT = 20 * 1024 * 1024


def lane_low(rows):
    return lax.broadcasted_iota(jnp.int32, (rows, LANES), 1) < 64


def swap_halves(value):
    return pltpu.roll(value, 64, 1)


def narrow_pack(wide, natural, out_ref, start, columns):
    full = columns // LANES
    period = 2 * full + 1
    pairs = PIECE_ROWS // period
    low = lane_low(pairs)
    part = [wide[pl.ds(start + j, pairs, stride=period), :] for j in range(period)]
    at = start
    for c in range(full):
        natural[pl.ds(0, pairs, stride=2), :] = part[c]
        natural[pl.ds(1, pairs, stride=2), :] = swap_halves(
            jnp.where(low, part[full + c + 1], part[full + c])
        )
        out_ref[at : at + 2 * pairs, :] = natural[0 : 2 * pairs, :].astype(jnp.bfloat16)
        at += 2 * pairs
    natural[pl.ds(0, pairs, stride=2), :] = part[full]
    natural[pl.ds(1, pairs, stride=2), :] = swap_halves(part[2 * full])
    out_ref[at : at + pairs, :] = jnp.where(
        low, natural[0:pairs, :], swap_halves(natural[pairs : 2 * pairs, :])
    ).astype(jnp.bfloat16)


def narrow_unpack(packed, natural, out_ref, start, columns):
    full = columns // LANES
    period = 2 * full + 1
    pairs = PIECE_ROWS // period
    low = lane_low(pairs)
    evens, odds = [], []
    at = start
    for c in range(full):
        natural[0 : 2 * pairs, :] = packed[at : at + 2 * pairs, :]
        evens.append(natural[pl.ds(0, pairs, stride=2), :])
        odds.append(swap_halves(natural[pl.ds(1, pairs, stride=2), :]))
        at += 2 * pairs
    tail = packed[at : at + pairs, :]
    natural[0:pairs, :] = tail
    natural[pairs : 2 * pairs, :] = swap_halves(tail)
    tail_even = natural[pl.ds(0, pairs, stride=2), :]
    tail_odd = swap_halves(natural[pl.ds(1, pairs, stride=2), :])
    rows = evens + [jnp.where(low, tail_even, odds[0])]
    for c in range(full - 1):
        rows.append(jnp.where(low, odds[c], odds[c + 1]))
    rows.append(jnp.where(low, odds[full - 1], tail_odd))
    for j in range(period):
        out_ref[pl.ds(start + j, pairs, stride=period), :] = rows[j]


def by_owner(owner, narrow, wide):
    @pl.when((owner == 0) | (owner == 3) | (owner >= 12))
    def _():
        narrow(0, D)
        narrow(PIECE_ROWS, D)

    @pl.when(owner == 1)
    def _():
        narrow(0, D)
        narrow(PIECE_ROWS, KV_HEADS * HEAD)

    @pl.when(owner == 2)
    def _():
        narrow(0, KV_HEADS * HEAD)
        narrow(PIECE_ROWS, D)

    @pl.when((owner >= 4) & (owner < 12))
    def _():
        wide()


def pack_kernel(owner_ref, flat_ref, gain_ref, *refs):
    count = len(GATHER_CUTS) - 1
    chunks = refs[:count]
    wide, natural, block = refs[count:]
    for number in range(SHARD_ROWS):
        wide[number : number + 1, :] = flat_ref[
            0:1, number * LANES : (number + 1) * LANES
        ].astype(jnp.float32)
    block[SHARD_ROWS:BLOCK_ROWS, :] = gain_ref[...]

    def narrow(start, columns):
        narrow_pack(wide, natural, block, start, columns)

    def broad():
        blocks = FF // LANES
        rows = SHARD_ROWS // blocks
        for c in range(blocks):
            block[c * rows : (c + 1) * rows, :] = wide[pl.ds(c, rows, stride=blocks), :].astype(
                jnp.bfloat16
            )

    by_owner(owner_ref[0], narrow, broad)
    for number in range(count):
        chunks[number][...] = block[GATHER_CUTS[number] : GATHER_CUTS[number + 1], :]


def pack_shard(owner, flat, gain_rows):
    sizes = [GATHER_CUTS[n + 1] - GATHER_CUTS[n] for n in range(len(GATHER_CUTS) - 1)]
    return pl.pallas_call(
        pack_kernel,
        out_shape=tuple(jax.ShapeDtypeStruct((size, LANES), jnp.bfloat16) for size in sizes),
        in_specs=[pl.BlockSpec(memory_space=pltpu.SMEM)] + in_vmem(2),
        out_specs=tuple(in_vmem(len(sizes))),
        scratch_shapes=[
            pltpu.VMEM((SHARD_ROWS, LANES), jnp.float32),
            pltpu.VMEM((1152, LANES), jnp.float32),
            pltpu.VMEM((BLOCK_ROWS, LANES), jnp.bfloat16),
        ],
        compiler_params=pltpu.CompilerParams(vmem_limit_bytes=VMEM_LIMIT),
        cost_estimate=pl.CostEstimate(flops=20_000_000_000, bytes_accessed=0, transcendentals=0),
    )(owner, flat, gain_rows)


def finish_kernel(owner_ref, *refs):
    count = len(REDUCE_CUTS) - 1
    kept_refs, got_refs = refs[:count], refs[count : 2 * count]
    out_ref, gain_ref, total, natural = refs[2 * count :]
    for number in range(count):
        total[REDUCE_CUTS[number] : REDUCE_CUTS[number + 1], :] = kept_refs[number][
            ...
        ].astype(jnp.float32) + got_refs[number][...].astype(jnp.float32)
    gain_ref[...] = total[SHARD_ROWS:, :]

    def narrow(start, columns):
        narrow_unpack(total, natural, out_ref, start, columns)

    def broad():
        blocks = FF // LANES
        rows = SHARD_ROWS // blocks
        for c in range(blocks):
            out_ref[pl.ds(c, rows, stride=blocks), :] = total[c * rows : (c + 1) * rows, :]

    by_owner(owner_ref[0], narrow, broad)


def in_vmem(count):
    return [pl.BlockSpec(memory_space=pltpu.VMEM)] * count


def finish_shard(owner, kept, got):
    return pl.pallas_call(
        finish_kernel,
        out_shape=(
            jax.ShapeDtypeStruct((SHARD_ROWS, LANES), jnp.float32),
            jax.ShapeDtypeStruct((GAIN_ROWS, LANES), jnp.float32),
        ),
        in_specs=[pl.BlockSpec(memory_space=pltpu.SMEM)] + in_vmem(len(kept) + len(got)),
        out_specs=tuple(in_vmem(2)),
        scratch_shapes=[
            pltpu.VMEM((BLOCK_ROWS, LANES), jnp.float32),
            pltpu.VMEM((1152, LANES), jnp.float32),
        ],
        compiler_params=pltpu.CompilerParams(vmem_limit_bytes=VMEM_LIMIT),
        cost_estimate=pl.CostEstimate(flops=20_000_000_000, bytes_accessed=0, transcendentals=0),
    )(owner, *kept, *got)


SLOTS = 1024
KEY_MAIN = 640
KEY_TAIL = 576
VALUE_MAIN = 768
VALUE_TAIL = 896
GATHER_CUTS = (0, 544, 1088, 1408, 1744)
GATHER_ORDERS = ((8, 4, 2, 1), (4, 8, 1, 2), (2, 1, 8, 4), (1, 2, 4, 8))
REDUCE_CUTS = (0, 320, 640, 1088, 1408, 1744)
REDUCE_ORDERS = (
    (1, 2, 4, 8),
    (2, 1, 4, 8),
    (4, 8, 1, 2),
    (1, 2, 4, 8),
    (2, 1, 4, 8),
)


def place_narrow(block, at, target, row, main, tail, columns):
    full = columns // LANES
    pairs = PIECE_ROWS // (2 * full + 1)
    for c in range(full):
        target[pl.ds(row, 2 * pairs), main + c * LANES : main + (c + 1) * LANES] = block[
            at : at + 2 * pairs, :
        ]
        at += 2 * pairs
    target[pl.ds(row, pairs), tail : tail + 64] = block[at : at + pairs, :64]
    target[pl.ds(row + pairs, pairs), tail : tail + 64] = block[at : at + pairs, 64:]


def place_kernel(index_ref, *refs):
    count = len(GATHER_CUTS) - 1
    chunks = refs[:count]
    joined, out, gate, up, down, gain, block = refs[count:]
    owner = pl.program_id(0)
    kv_width = KV_HEADS * HEAD
    for number in range(count):
        block[GATHER_CUTS[number] : GATHER_CUTS[number + 1], :] = chunks[number][
            index_ref[number, owner]
        ]
    gain[pl.ds(pl.multiple_of(owner * GAIN_ROWS, GAIN_ROWS), GAIN_ROWS), :] = block[SHARD_ROWS:, :]

    @pl.when(owner == 0)
    def _():
        joined[:, SLOTS - 128 :] = jnp.zeros((D, 128), jnp.bfloat16)
        place_narrow(block, 0, joined, 0, 0, 512, D)
        place_narrow(block, PIECE_ROWS, joined, 192, 0, 512, D)

    @pl.when(owner == 1)
    def _():
        place_narrow(block, 0, joined, 384, 0, 512, D)
        place_narrow(block, PIECE_ROWS, joined, 0, KEY_MAIN, KEY_TAIL, kv_width)

    @pl.when(owner == 2)
    def _():
        place_narrow(block, 0, joined, 0, VALUE_MAIN, VALUE_TAIL, kv_width)
        place_narrow(block, PIECE_ROWS, out, 0, 0, 512, D)

    @pl.when(owner == 3)
    def _():
        place_narrow(block, 0, out, 192, 0, 512, D)
        place_narrow(block, PIECE_ROWS, out, 384, 0, 512, D)

    def broad(target, first):
        @pl.when((owner >= first) & (owner < first + 4))
        def _():
            row = pl.multiple_of((owner - first) * 144, 16)
            for c in range(FF // LANES):
                target[pl.ds(row, 144), c * LANES : (c + 1) * LANES] = block[
                    c * 144 : (c + 1) * 144, :
                ]

    broad(gate, 4)
    broad(up, 8)

    @pl.when(owner >= 12)
    def _():
        row = pl.multiple_of((owner - 12) * 384, 16)
        place_narrow(block, 0, down, row, 0, 512, D)
        place_narrow(block, PIECE_ROWS, down, pl.multiple_of(row + 192, 16), 0, 512, D)


def place_blocks(index, chunks):
    shapes = [(D, SLOTS), (D, D), (D, FF), (D, FF), (FF, D), (16 * GAIN_ROWS, LANES)]
    return pl.pallas_call(
        place_kernel,
        out_shape=tuple(jax.ShapeDtypeStruct(shape, jnp.bfloat16) for shape in shapes),
        grid=(16,),
        in_specs=[pl.BlockSpec(memory_space=pltpu.SMEM)] + in_vmem(len(chunks)),
        out_specs=tuple(in_vmem(len(shapes))),
        scratch_shapes=[pltpu.VMEM((BLOCK_ROWS, LANES), jnp.bfloat16)],
        compiler_params=pltpu.CompilerParams(vmem_limit_bytes=VMEM_LIMIT),
        cost_estimate=pl.CostEstimate(flops=20_000_000_000, bytes_accessed=0, transcendentals=0),
    )(index, *chunks)


def store_narrow(result, block, at, main, tail, columns):
    full = columns // LANES
    pairs = PIECE_ROWS // (2 * full + 1)
    for c in range(full):
        block[at : at + 2 * pairs, :] = result[
            :, main + c * LANES : main + (c + 1) * LANES
        ].astype(jnp.bfloat16)
        at += 2 * pairs
    block[at : at + pairs, :] = jnp.concatenate(
        [result[:pairs, tail : tail + 64], result[pairs:, tail : tail + 64]], axis=1
    ).astype(jnp.bfloat16)


def deal_block(index_ref, halves, block, owner):
    for number in range(len(REDUCE_CUTS) - 1):
        first, last = REDUCE_CUTS[number], REDUCE_CUTS[number + 1]
        place = index_ref[number, owner]

        @pl.when(place < 8)
        def _():
            halves[2 * number][place] = block[first:last, :]

        @pl.when(place >= 8)
        def _():
            halves[2 * number + 1][place - 8] = block[first:last, :]


def turned_product(turned_ref, row, count, right):
    return jnp.dot(turned_ref[row : row + count, :], right, preferred_element_type=jnp.float32)


def wide_terms_kernel(
    attended,
    normed_two,
    hidden,
    grad_mixed,
    grad_gate,
    grad_up,
    grad_output,
    blocks,
    attended_t,
    normed_two_t,
    hidden_t,
):
    normed_two_t[...] = normed_two[...].T
    for number, right in ((0, grad_gate), (1, grad_up)):
        for part in range(4):
            result = turned_product(normed_two_t, 144 * part, 144, right[...]).astype(jnp.bfloat16)
            for c in range(FF // LANES):
                blocks[1 + 4 * number + part, c * 144 : (c + 1) * 144, :] = lanes(result, c)
    hidden_t[...] = hidden[...].T
    for part in range(4):
        block = blocks.at[9 + part]
        for half in range(2):
            result = turned_product(hidden_t, 384 * part + 192 * half, 192, grad_output[...])
            store_narrow(result, block, half * PIECE_ROWS, 0, 512, D)
    attended_t[...] = attended[...].T
    block = blocks.at[0]
    for half in range(2):
        result = turned_product(attended_t, 192 + 192 * half, 192, grad_mixed[...])
        store_narrow(result, block, half * PIECE_ROWS, 0, 512, D)


def narrow_terms_kernel(index_ref, normed, attended, grad_joined, grad_mixed, gain_ref, *refs):
    wide_blocks = refs[0]
    *halves, block, normed_t, attended_t = refs[1:]
    kv_width = KV_HEADS * HEAD
    normed_t[...] = normed[...].T
    attended_t[...] = attended[...].T
    query = grad_joined[:, :KEY_MAIN]
    for owner in range(16):
        block[SHARD_ROWS:BLOCK_ROWS, :] = gain_ref[owner]
        if owner == 0:
            for half in range(2):
                result = turned_product(normed_t, 192 * half, 192, query)
                store_narrow(result, block, half * PIECE_ROWS, 0, 512, D)
        elif owner == 1:
            store_narrow(turned_product(normed_t, 384, 192, query), block, 0, 0, 512, D)
            key = turned_product(normed_t, 0, D, grad_joined[:, 512:768])
            store_narrow(key, block, PIECE_ROWS, KEY_MAIN - 512, KEY_TAIL - 512, kv_width)
        elif owner == 2:
            value = turned_product(normed_t, 0, D, grad_joined[:, VALUE_MAIN:])
            store_narrow(value, block, 0, 0, VALUE_TAIL - VALUE_MAIN, kv_width)
            result = turned_product(attended_t, 0, 192, grad_mixed[...])
            store_narrow(result, block, PIECE_ROWS, 0, 512, D)
        else:
            block[:SHARD_ROWS, :] = wide_blocks[owner - 3]
        deal_block(index_ref, halves, block, owner)


def wide_terms(factors):
    rows = factors[0].shape[0]
    return on_core(
        wide_terms_kernel,
        [((13, SHARD_ROWS, LANES), jnp.bfloat16)],
        [
            pltpu.VMEM((D, rows), jnp.bfloat16),
            pltpu.VMEM((D, rows), jnp.bfloat16),
            pltpu.VMEM((FF, rows), jnp.bfloat16),
        ],
        *factors,
    )[0]


def narrow_terms(index, factors, gain_rows, wide_blocks):
    shapes = tuple(
        jax.ShapeDtypeStruct((8, REDUCE_CUTS[n + 1] - REDUCE_CUTS[n], LANES), jnp.bfloat16)
        for n in range(len(REDUCE_CUTS) - 1)
        for _ in range(2)
    )
    rows = factors[0].shape[0]
    return pl.pallas_call(
        narrow_terms_kernel,
        out_shape=shapes,
        in_specs=[pl.BlockSpec(memory_space=pltpu.SMEM)] + in_vmem(len(factors) + 2),
        out_specs=tuple(in_vmem(len(shapes))),
        scratch_shapes=[
            pltpu.VMEM((BLOCK_ROWS, LANES), jnp.bfloat16),
            pltpu.VMEM((D, rows), jnp.bfloat16),
            pltpu.VMEM((D, rows), jnp.bfloat16),
        ],
        compiler_params=pltpu.CompilerParams(vmem_limit_bytes=VMEM_LIMIT),
        cost_estimate=pl.CostEstimate(flops=20_000_000_000, bytes_accessed=0, transcendentals=0),
    )(index, *factors, gain_rows, wide_blocks)


def partner(value, stride):
    count = lax.axis_size("fsdp")
    return lax.ppermute(value, "fsdp", [(source, source ^ stride) for source in range(count)])


def block_index(orders, first_is_low):
    apart = jnp.arange(16, dtype=jnp.int32) ^ lax.axis_index("fsdp").astype(jnp.int32)
    rows = []
    for order in orders:
        place = jnp.zeros_like(apart)
        for stage, stride in enumerate(order):
            bit = stage if first_is_low else len(order) - 1 - stage
            place = place + jnp.where((apart & stride) != 0, 1 << bit, 0)
        rows.append(place)
    return jnp.stack(rows)


def gather_layer(weights, gains, segments):
    owners = lax.axis_size("fsdp")
    if owners != 16:
        flat_full = lax.all_gather(weights[0], "fsdp", axis=0, tiled=True)
        gain_full = lax.all_gather(gains[0], "fsdp", axis=0, tiled=True)
        query, key, value, out, gate, up, down = unpack(flat_full)
        joined = jnp.concatenate(
            [
                query,
                key[:, LANES:],
                key[:, :LANES],
                value,
                jnp.zeros((D, SLOTS - VALUE_TAIL - 64), jnp.bfloat16),
            ],
            axis=1,
        )
        return (joined, out, gate, up, down), gain_full.astype(jnp.float32).reshape(2, D), segments
    owner = lax.axis_index("fsdp").astype(jnp.int32).reshape(1)
    share = gains.shape[1]
    gain_rows = jnp.pad(gains, ((0, GAIN_ROWS - 1), (0, LANES - share)))
    chunks = list(pack_shard(owner, weights, gain_rows))
    segments, *chunks = lax.optimization_barrier((segments, *chunks))
    for stage in range(4):
        got = [partner(chunk, order[stage]) for chunk, order in zip(chunks, GATHER_ORDERS)]
        chunks = [jnp.concatenate(both) for both in zip(chunks, got)]
    chunks = [chunk.reshape(16, -1, LANES) for chunk in chunks]
    *mats, gain_full = place_blocks(block_index(GATHER_ORDERS, True), chunks)
    gain_full = gain_full.reshape(16, GAIN_ROWS, LANES)[:, 0, :share]
    return tuple(mats), gain_full.astype(jnp.float32).reshape(2, D), segments


def reduce_terms(factors, gain_grad, wide_blocks):
    owners = lax.axis_size("fsdp")
    share = gain_grad.shape[0] // owners
    if owners != 16:
        normed, attended, normed_two, hidden, joined, grad_mixed, grad_gate, grad_up, last = factors
        pairs = [
            (normed, joined[:, :D]),
            (normed, jnp.concatenate([joined[:, KEY_MAIN:VALUE_MAIN], joined[:, D:KEY_MAIN]], 1)),
            (normed, joined[:, VALUE_MAIN : VALUE_TAIL + 64]),
            (attended, grad_mixed),
            (normed_two, grad_gate),
            (normed_two, grad_up),
            (hidden, last),
        ]
        flat_grads = jnp.concatenate(
            [
                jnp.einsum("rd,re->de", left, right, preferred_element_type=jnp.float32).reshape(-1)
                for left, right in pairs
            ]
        )
        got = [
            lax.all_to_all(
                item.reshape(owners, -1).astype(jnp.bfloat16),
                "fsdp",
                split_axis=0,
                concat_axis=0,
                tiled=True,
            ).astype(jnp.float32)
            for item in (flat_grads, gain_grad)
        ]
        return tuple(jnp.sum(item, axis=0) for item in got)
    gain_rows = jnp.pad(
        gain_grad.reshape(owners, 1, share).astype(jnp.bfloat16),
        ((0, 0), (0, GAIN_ROWS - 1), (0, LANES - share)),
    )
    normed, attended, _, _, grad_joined, grad_mixed = factors[:6]
    halves = narrow_terms(
        block_index(REDUCE_ORDERS, False),
        (normed, attended, grad_joined, grad_mixed),
        gain_rows,
        wide_blocks,
    )
    kept, sent = halves[0::2], halves[1::2]
    for stage in range(4):
        if stage:
            half = 8 >> stage
            kept, sent = [item[:half] for item in sums], [item[half:] for item in sums]
        got = [partner(item, order[stage]) for item, order in zip(sent, REDUCE_ORDERS)]
        if stage < 3:
            sums = [
                (one.astype(jnp.float32) + other.astype(jnp.float32)).astype(jnp.bfloat16)
                for one, other in zip(kept, got)
            ]
    owner = lax.axis_index("fsdp").astype(jnp.int32).reshape(1)
    flat, gain = finish_shard(owner, [item[0] for item in kept], [item[0] for item in got])
    return flat.reshape(-1), gain[0, :share]


def turned(block, cosine, sine):
    low = lax.broadcasted_iota(jnp.int32, block.shape, 1) % 64 < 32
    other = jnp.where(low, pltpu.roll(block, 96, 1), pltpu.roll(block, 32, 1))
    return block * cosine + other * sine


def lanes(value, number):
    return value[:, number * LANES : (number + 1) * LANES]


def project_kernel(states_ref, gain, joined, cosine, sine, normed, query, pair):
    states = states_ref[...].astype(jnp.float32)
    low_rows = (states * rms_scale(states) * gain[0:1, :]).astype(jnp.bfloat16)
    normed[...] = low_rows
    full = jnp.dot(low_rows, joined[...], preferred_element_type=jnp.float32)
    blocks = [turned(lanes(full, number), cosine[...], sine[...]) for number in range(6)]
    for number in range(5):
        query[:, number * LANES : (number + 1) * LANES] = blocks[number].astype(jnp.bfloat16)
    low = lane_low(full.shape[0])
    pair[:, :LANES] = blocks[5].astype(jnp.bfloat16)
    pair[:, LANES : 2 * LANES] = lanes(full, 6).astype(jnp.bfloat16)
    pair[:, 2 * LANES :] = jnp.where(
        low, swap_halves(blocks[4]), swap_halves(lanes(full, 7))
    ).astype(jnp.bfloat16)


KEY_AT = (0, 64, 256)
VALUE_AT = (128, 192, 320)


def fill_window(window, pieces):
    micro_count, span, _ = window.shape
    rows = span // len(pieces)
    for micro in range(micro_count):
        for number, piece in enumerate(pieces):
            window[micro, number * rows : (number + 1) * rows, :] = piece[
                micro * rows : (micro + 1) * rows, :
            ]


def stacked_heads(ref, micro, rows, kv_head):
    group = HEADS // KV_HEADS
    return jnp.concatenate(
        [
            ref[micro * rows : (micro + 1) * rows, head * HEAD : (head + 1) * HEAD]
            for head in range(kv_head * group, (kv_head + 1) * group)
        ],
        axis=0,
    )


def shares_of(queries, keys, bias):
    scores = lax.dot_general(
        queries, keys, (((1,), (1,)), ((), ())), preferred_element_type=jnp.float32
    ) * HEAD ** (-0.5)
    group = HEADS // KV_HEADS
    rows, span = bias.shape
    scores = scores.reshape(group, rows, span) + bias[None]
    powers = jnp.exp(scores - jnp.max(scores, axis=-1, keepdims=True))
    shares = powers / jnp.sum(powers, axis=-1, keepdims=True)
    return shares.reshape(group * rows, span)


def forward_kernel(
    states,
    query,
    pair_two,
    pair_one,
    pair_own,
    bias,
    gain,
    w_out,
    w_gate,
    w_up,
    w_down,
    output,
    *refs,
):
    if len(refs) == 7:
        attended, mixed, normed_two, gate, up, hidden, window = refs
    else:
        attended, mixed, hidden, window = refs
        normed_two = gate = up = None
    group = HEADS // KV_HEADS
    fill_window(window, (pair_two, pair_one, pair_own))
    micro_count, rows, _ = bias.shape
    for micro in range(micro_count):
        for kv_head in range(KV_HEADS):
            keys = window[micro, :, KEY_AT[kv_head] : KEY_AT[kv_head] + HEAD]
            values = window[micro, :, VALUE_AT[kv_head] : VALUE_AT[kv_head] + HEAD]
            shares = shares_of(stacked_heads(query, micro, rows, kv_head), keys, bias[micro])
            got = jnp.dot(
                shares.astype(jnp.bfloat16), values, preferred_element_type=jnp.float32
            ).astype(jnp.bfloat16)
            for number in range(group):
                head = kv_head * group + number
                attended[micro * rows : (micro + 1) * rows, head * HEAD : (head + 1) * HEAD] = got[
                    number * rows : (number + 1) * rows, :
                ]
    middle = states[...].astype(jnp.float32) + jnp.dot(
        attended[...], w_out[...], preferred_element_type=jnp.float32
    )
    mixed[...] = middle
    low_rows = (middle * rms_scale(middle) * gain[1:2, :]).astype(jnp.bfloat16)
    if normed_two is not None:
        normed_two[...] = low_rows
    width = FF // 3
    for part in range(3):
        at = slice(part * width, (part + 1) * width)
        gates = jnp.dot(low_rows, w_gate[:, at], preferred_element_type=jnp.float32)
        ups = jnp.dot(low_rows, w_up[:, at], preferred_element_type=jnp.float32)
        if gate is not None:
            gate[:, at] = gates
            up[:, at] = ups
        hidden[:, at] = (gates * jax.nn.sigmoid(gates) * ups).astype(jnp.bfloat16)
    output[...] = (
        mixed[...] + jnp.dot(hidden[...], w_down[...], preferred_element_type=jnp.float32)
    ).astype(jnp.bfloat16)


def against(left, right):
    return lax.dot_general(left, right, (((1,), (1,)), ((), ())), preferred_element_type=jnp.float32)


def across(left, right):
    return lax.dot_general(left, right, (((0,), (0,)), ((), ())), preferred_element_type=jnp.float32)


def backward_kernel(
    grad_output,
    query,
    pair_two,
    pair_one,
    pair_own,
    bias,
    gain,
    mixed,
    gate,
    up,
    w_out,
    w_gate,
    w_up,
    w_down,
    grad_mixed,
    grad_query,
    grad_two,
    grad_one,
    grad_own,
    *refs,
):
    if len(refs) == 6:
        grad_gate, grad_up, grad_mixed_low, gain_grad, window, grad_attended = refs
    else:
        grad_gate, grad_up, window, grad_attended = refs
        grad_mixed_low = gain_grad = None
    group = HEADS // KV_HEADS
    fill_window(window, (pair_two, pair_one, pair_own))
    width = FF // 3
    grads = grad_output[...]
    for part in range(3):
        at = slice(part * width, (part + 1) * width)
        grad_hidden = against(grads, w_down[at, :])
        gates = gate[:, at]
        sigmoid = jax.nn.sigmoid(gates)
        grad_gate[:, at] = (
            grad_hidden * up[:, at] * sigmoid * (1.0 + gates * (1.0 - sigmoid))
        ).astype(jnp.bfloat16)
        grad_up[:, at] = (grad_hidden * gates * sigmoid).astype(jnp.bfloat16)
    grad_normed = against(grad_gate[...], w_gate[...]) + against(grad_up[...], w_up[...])
    middle = mixed[...]
    scale = rms_scale(middle)
    if gain_grad is not None:
        gain_grad[...] = jnp.broadcast_to(
            jnp.sum(middle * scale * grad_normed, axis=0, keepdims=True), gain_grad.shape
        )
    grad_middle = grads.astype(jnp.float32) + rms_back(middle, scale, gain[1:2, :], grad_normed)
    grad_mixed[...] = grad_middle
    low_rows = grad_middle.astype(jnp.bfloat16)
    if grad_mixed_low is not None:
        grad_mixed_low[...] = low_rows
    grad_attended[...] = against(low_rows, w_out[...]).astype(jnp.bfloat16)
    micro_count, rows, _ = bias.shape
    for micro in range(micro_count):
        here = slice(micro * rows, (micro + 1) * rows)
        for kv_head in range(KV_HEADS):
            key_at = slice(KEY_AT[kv_head], KEY_AT[kv_head] + HEAD)
            value_at = slice(VALUE_AT[kv_head], VALUE_AT[kv_head] + HEAD)
            keys = window[micro, :, key_at]
            values = window[micro, :, value_at]
            queries = stacked_heads(query, micro, rows, kv_head)
            coming = stacked_heads(grad_attended, micro, rows, kv_head)
            shares = shares_of(queries, keys, bias[micro])
            grad_shares = against(coming, values)
            inner = jnp.sum(shares * grad_shares, axis=-1, keepdims=True)
            grad_scores = (shares * (grad_shares - inner)).astype(jnp.bfloat16)
            got = jnp.dot(grad_scores, keys, preferred_element_type=jnp.float32) * HEAD ** (-0.5)
            for number in range(group):
                head = kv_head * group + number
                grad_query[here, head * HEAD : (head + 1) * HEAD] = got[
                    number * rows : (number + 1) * rows, :
                ]
            grad_keys = across(grad_scores, queries) * HEAD ** (-0.5)
            grad_values = across(shares.astype(jnp.bfloat16), coming)
            for lane_at, item in ((key_at, grad_keys), (value_at, grad_values)):
                grad_two[here, lane_at] = item[:rows].astype(jnp.bfloat16)
                grad_one[here, lane_at] = item[rows : 2 * rows].astype(jnp.bfloat16)
                grad_own[here, lane_at] = item[2 * rows :]


def close_kernel(
    states_ref,
    grad_query,
    grad_own,
    got_one,
    got_two,
    grad_mixed,
    cosine,
    sine,
    gain,
    joined,
    grad_states,
    grad_joined,
    *refs,
):
    pair = (
        grad_own[...]
        + got_one[...].astype(jnp.float32)
        + got_two[...].astype(jnp.float32)
    )
    low = lane_low(pair.shape[0])
    tail = swap_halves(lanes(pair, 2))
    blocks = [grad_query[:, number * LANES : (number + 1) * LANES] for number in range(5)]
    blocks[4] = jnp.where(low, blocks[4], tail)
    blocks.append(lanes(pair, 0))
    back = -sine[...]
    blocks = [turned(block, cosine[...], back) for block in blocks]
    blocks.append(lanes(pair, 1))
    blocks.append(jnp.where(low, tail, 0.0))
    for number, block in enumerate(blocks):
        grad_joined[:, number * LANES : (number + 1) * LANES] = block.astype(jnp.bfloat16)
    grad_normed = against(grad_joined[...], joined[...])
    states = states_ref[...].astype(jnp.float32)
    scale = rms_scale(states)
    for gain_grad in refs:
        gain_grad[...] = jnp.broadcast_to(
            jnp.sum(states * scale * grad_normed, axis=0, keepdims=True), gain_grad.shape
        )
    grad_states[...] = (
        grad_mixed[...] + rms_back(states, scale, gain[0:1, :], grad_normed)
    ).astype(jnp.bfloat16)


def on_core(kernel, shapes, scratch, *operands):
    return pl.pallas_call(
        kernel,
        out_shape=tuple(jax.ShapeDtypeStruct(shape, dtype) for shape, dtype in shapes),
        in_specs=in_vmem(len(operands)),
        out_specs=tuple(in_vmem(len(shapes))),
        scratch_shapes=scratch,
        compiler_params=pltpu.CompilerParams(vmem_limit_bytes=VMEM_LIMIT),
        cost_estimate=pl.CostEstimate(flops=20_000_000_000, bytes_accessed=0, transcendentals=0),
    )(*operands)


def layer_forward(states, mats, gain_pair, tables, keep):
    joined, w_out, w_gate, w_up, w_down = mats
    cosine, sine, bias = tables
    rows = states.shape[0]
    low, wide = jnp.bfloat16, jnp.float32
    normed, query, pair = on_core(
        project_kernel,
        [((rows, D), low), ((rows, KEY_MAIN), low), ((rows, 3 * LANES), low)],
        [],
        states,
        gain_pair,
        joined,
        cosine,
        sine,
    )
    window = (passed_along(pair, "fsdp", 2), passed_along(pair, "fsdp", 1), pair)
    window_space = pltpu.VMEM((bias.shape[0], bias.shape[2], 3 * LANES), low)
    shapes = [
        ((rows, D), low),
        ((rows, D), low),
        ((rows, D), wide),
        ((rows, D), low),
        ((rows, FF), wide),
        ((rows, FF), wide),
        ((rows, FF), low),
    ]
    spaces = [pltpu.VMEM(*shapes[number]) for number in (1, 2, 6)]
    output, *kept = on_core(
        forward_kernel,
        shapes if keep else shapes[:1],
        [window_space] if keep else spaces + [window_space],
        states,
        query,
        *window,
        bias,
        gain_pair,
        w_out,
        w_gate,
        w_up,
        w_down,
    )
    return output, (normed, query, window, *kept)


def layer_backward(grad_output, states, kept, mats, gain_pair, tables, keep):
    joined, w_out, w_gate, w_up, w_down = mats
    cosine, sine, bias = tables
    normed, query, window, attended, mixed, normed_two, gate, up, hidden = kept
    rows = states.shape[0]
    low, wide = jnp.bfloat16, jnp.float32
    pair_shape = (rows, 3 * LANES)
    shapes = [
        ((rows, D), wide),
        ((rows, KEY_MAIN), wide),
        (pair_shape, low),
        (pair_shape, low),
        (pair_shape, wide),
    ]
    more = [((rows, FF), low), ((rows, FF), low), ((rows, D), low), ((8, D), wide)]
    spaces = [
        pltpu.VMEM((bias.shape[0], bias.shape[2], 3 * LANES), low),
        pltpu.VMEM((rows, D), low),
    ]
    if not keep:
        spaces = [pltpu.VMEM(*shape) for shape in more[:2]] + spaces
    grad_mixed, grad_query, grad_two, grad_one, grad_own, *record = on_core(
        backward_kernel,
        shapes + more if keep else shapes,
        spaces,
        grad_output,
        query,
        *window,
        bias,
        gain_pair,
        mixed,
        gate,
        up,
        w_out,
        w_gate,
        w_up,
        w_down,
    )
    got_one = passed_along(grad_one, "fsdp", -1)
    got_two = passed_along(grad_two, "fsdp", -2)
    operands = (
        states,
        grad_query,
        grad_own,
        got_one,
        got_two,
        grad_mixed,
        cosine,
        sine,
        gain_pair,
        joined,
    )
    if not keep:
        return on_core(
            close_kernel, [((rows, D), low)], [pltpu.VMEM((rows, SLOTS), low)], *operands
        )[0]
    grad_states, grad_joined, gain_one = on_core(
        close_kernel, [((rows, D), low), ((rows, SLOTS), low), ((8, D), wide)], [], *operands
    )
    wide_blocks = None
    if keep and lax.axis_size("fsdp") == 16:
        last, grad_states = lax.optimization_barrier((grad_output, grad_states))
        wide_blocks = wide_terms(
            (attended, normed_two, hidden, record[2], record[0], record[1], last)
        )
    grad_gate, grad_up, grad_mixed_low, gain_two = record
    factors = (
        normed,
        attended,
        normed_two,
        hidden,
        grad_joined,
        grad_mixed_low,
        grad_gate,
        grad_up,
        grad_output,
    )
    return grad_states, factors, jnp.concatenate([gain_one[0], gain_two[0]]), wide_blocks


def local(ends, weights, gains, segments):
    micro_count = ends.shape[1]
    rows = ends.shape[2]
    first = lax.axis_index("section") == 0
    mats, gain_pair, segments = gather_layer(weights, gains, segments)
    marked = segments + 1
    rims = [passed_along(marked, "fsdp", 2), passed_along(marked, "fsdp", 1), marked]
    window_segments = jnp.concatenate(rims, axis=1)
    span = window_segments.shape[1]
    place = jnp.arange(span, dtype=jnp.int32)
    change = jnp.concatenate(
        [jnp.ones((micro_count, 1), dtype=bool), window_segments[:, 1:] != window_segments[:, :-1]],
        axis=1,
    )
    starts = lax.cummax(jnp.where(change, place[None, :], 0), axis=1)
    positions = (place[None, :] - starts)[:, span - rows :].reshape(-1)
    cosine, sine = rope_tables(positions)
    cosine = jnp.concatenate([cosine] * 4, axis=1)
    sine = jnp.concatenate([-sine, sine, -sine, sine], axis=1)
    allowed = (window_segments[:, span - rows :, None] == window_segments[:, None, :]) & (
        place[None, None, :] <= place[None, span - rows :, None]
    )
    bias = jnp.where(allowed, 0.0, masked_score).astype(jnp.float32)
    tables = (cosine, sine, bias)
    own = ends[0].reshape(micro_count * rows, D)
    middle, _ = layer_forward(own, mats, gain_pair, tables, False)
    states = jnp.where(first, own, passed_along(middle, "section", 1))
    output, kept = layer_forward(states, mats, gain_pair, tables, True)
    grad_middle = layer_backward(own, states, kept, mats, gain_pair, tables, False)
    grad_output = jnp.where(first, passed_along(grad_middle, "section", -1), own)
    grad_states, factors, gain_grad, wide_blocks = layer_backward(
        grad_output, states, kept, mats, gain_pair, tables, True
    )
    weight_share, gain_share = reduce_terms(factors, gain_grad, wide_blocks)
    ends_out = jnp.where(first, grad_states, output).reshape(ends.shape)
    return (ends_out, weight_share[None], gain_share[None])


def solution(mesh):
    placed = (
        P("section", None, "fsdp", None),
        P("section", "fsdp"),
        P("section", "fsdp"),
        P(None, "fsdp"),
    )
    return jax.shard_map(
        local,
        mesh=mesh,
        in_specs=placed,
        out_specs=(P("section", None, "fsdp", None), P("section", "fsdp"), P("section", "fsdp")),
        check_vma=False,
    )
```
